256 devices in a mesh: freq: 64 (over z, y, core), tm: 4 (over x).
Axes of the slice: x: 4, y: 4, z: 8, core: 2. Of those that a mesh axis runs over, the one named last changes fastest.
Arguments:
- filterbank: float32 [4096, 8192], P('freq', 'tm'), may hold values from -6 to 6
- low_rows: int32 [9, 4096], P(None, 'freq'), may hold values from 0 to 63, as said below
- high_rows: int32 [9, 4096], P(None, 'freq'), may hold values from 0 to 63, as said below
- delays: int32 [9, 4096], P(None, 'freq'), may hold values from 0 to 256, as said below
Outputs:
- dm_transform: float32 [4096, 8192], P('freq', 'tm')
The draws below stay inside these ranges and needn't reach their ends.
Inputs may be any that keep to these rules, and one draw needn't show every extreme that they name: `low_rows`: at a level i below 6 an entry is below 2^i, at a level across owners below 64. The first row of every output sub-band takes row 0, its last row the largest allowed. `high_rows`: at a level i below 6 an entry is below 2^i, at a level across owners below 64. The first row of every output sub-band takes row 0, its last row the largest allowed. `delays`: at level i an entry is at most min(2^i, 512); the first row of every output sub-band has delay 0, its last row that bound.
All inputs are finite; a program needn't handle non-finite values.
Results may differ from the reference program's by a relative error of at most 0.00002.
Values sent between devices are 32-bit elements; how exact they have to be, the bound alone decides.
No kernel may reach another device: no remote copies, remote signals or barrier semaphores. Data moves between devices by JAX's collectives and lax.ppermute only.
A program may use at most 128 MiB of HBM per device.

```python
import math
import jax
import jax.numpy as jnp
from jax import lax

CH_DEV = 64
LOCAL = 6
LEVELS = 9
T_DEV = 2048
CHANNELS = 4096
TIME = 8192


def level_layout(merge_step):
    row_ids = jnp.arange(CHANNELS, dtype=jnp.int32)
    if merge_step < LOCAL:
        band_span = 2 ** (merge_step + 1)
        source_count = 2 ** merge_step
    else:
        band_span = CH_DEV
        source_count = CH_DEV
    return (row_ids % band_span, band_span, source_count)


def row_table(key):
    tables = []
    for merge_step in range(LEVELS):
        offset, band_span, source_count = level_layout(merge_step)
        picked = jax.random.randint(jax.random.fold_in(key, merge_step), (CHANNELS,), 0, source_count, dtype=jnp.int32)
        picked = jnp.where(offset == band_span - 1, source_count - 1, picked)
        picked = jnp.where(offset == 0, 0, picked)
        tables.append(picked.astype(jnp.int32))
    return jnp.stack(tables)


def draw_low_rows(key, part):
    key = jax.random.fold_in(key, 5)
    return row_table(key)


def draw_high_rows(key, part):
    key = jax.random.fold_in(key, 6)
    return row_table(key)


def draw_delays(key, part):
    key = jax.random.fold_in(key, 7)
    tables = []
    for merge_step in range(LEVELS):
        offset, band_span, source_count = level_layout(merge_step)
        lag_bound = min(2 ** merge_step, T_DEV // 4)
        picked = jax.random.randint(jax.random.fold_in(key, merge_step), (CHANNELS,), 0, lag_bound + 1, dtype=jnp.int32)
        picked = jnp.where(offset == band_span - 1, lag_bound, picked)
        picked = jnp.where(offset == 0, 0, picked)
        tables.append(picked.astype(jnp.int32))
    return jnp.stack(tables)


def block_levels(stream_key, shape, pieces, low, largest):
    gain, own = 1.0, jax.random.fold_in(stream_key, 6)
    for axis_at, shards_of in pieces:
        heights = jnp.exp(jax.random.uniform(jax.random.fold_in(own, axis_at), (shards_of,), jnp.float32, low / len(pieces), largest / len(pieces)))
        gain = gain * jnp.repeat(heights, shape[axis_at] // shards_of).reshape([-1 if axis == axis_at else 1 for axis in range(len(shape))])
    return gain


def normal_values(rng, extent, scale, most, split=(), held_as=jnp.bfloat16):
    drawn = scale * jax.random.normal(rng, extent, jnp.float32)
    if split:
        drawn = drawn * block_levels(rng, extent, split, -0.22, 0.18)
    return jnp.clip(drawn, -most, most).astype(held_as)


def setup_inputs(seed: int = 0) -> dict:
    streams_of = jax.random.split(jax.random.key(seed), 5)
    return {
        "filterbank": normal_values(streams_of[0], (CHANNELS, TIME), 1.0, 6.0, ((0, 64), (1, 4)), jnp.float32),
        "low_rows": draw_low_rows(jax.random.fold_in(streams_of[4], 71), 0),
        "high_rows": draw_high_rows(jax.random.fold_in(streams_of[4], 71), 0),
        "delays": draw_delays(jax.random.fold_in(streams_of[4], 71), 0),
    }


def level_sources(merge_step, low_rows, high_rows):
    row_ids = jnp.arange(CHANNELS, dtype=jnp.int32)
    if merge_step < LOCAL:
        band_span = 2 ** (merge_step + 1)
        band_start = row_ids - row_ids % band_span
        return (band_start + low_rows[merge_step], band_start + band_span // 2 + high_rows[merge_step])
    stride = 2 ** (merge_step - LOCAL)
    owner_ids = row_ids // CH_DEV
    lower_ids = owner_ids - jnp.bitwise_and(owner_ids, stride)
    return (lower_ids * CH_DEV + low_rows[merge_step], (lower_ids + stride) * CH_DEV + high_rows[merge_step])

def merge_level(spectra, low_idx, high_idx, lag_rows, lag_bound):
    series_len = spectra.shape[1]

    def one_block(block_tuple):
        low_blk, high_blk, lag_blk = block_tuple
        low_part = jnp.take(spectra, low_blk, axis=0)
        high_part = jnp.take(spectra, high_blk, axis=0)
        padded = jnp.concatenate([jnp.zeros((high_part.shape[0], lag_bound), jnp.float32), high_part], axis=1)
        moved = jax.vmap(lambda series, shift_by: lax.dynamic_slice_in_dim(series, lag_bound - shift_by, series_len))(padded, lag_blk)
        return low_part + moved
    block_tuple = (low_idx.reshape(-1, CH_DEV), high_idx.reshape(-1, CH_DEV), lag_rows.reshape(-1, CH_DEV))
    return lax.map(one_block, block_tuple).reshape(spectra.shape)

def reference(filterbank, low_rows, high_rows, delays):
    spectra = filterbank
    for merge_step in range(LEVELS):
        lag_bound = min(2 ** merge_step, T_DEV // 4)
        low_idx, high_idx = level_sources(merge_step, low_rows, high_rows)
        spectra = merge_level(spectra, low_idx, high_idx, delays[merge_step], lag_bound)
    return spectra * (1.0 / math.sqrt(2.0 ** LEVELS))
```

```python
import functools
import math

import jax
import jax.numpy as jnp
from jax import lax
from jax.experimental import pallas as pl
from jax.experimental.pallas import tpu as pltpu
from jax.sharding import PartitionSpec as P

LOCAL = 6
LEVELS = 9
ROWS = 64
LANES = 128
CHUNKS = 16
HALO = 4
GUARD = 8
SCALE = 1.0 / math.sqrt(2.0**LEVELS)
F32 = jnp.float32


def vmem_spec():
    return pl.BlockSpec(memory_space=pltpu.VMEM)


def smem_spec():
    return pl.BlockSpec(memory_space=pltpu.SMEM)


def in_vmem(value):
    return pltpu.with_memory_space_constraint(value, pltpu.VMEM)


def lanes(count):
    return lax.broadcasted_iota(jnp.int32, (count, LANES), 1)


def delayed(src, base, lag, count):
    start = base - lax.shift_right_logical(lag, 7)
    turn = jnp.bitwise_and(lag, LANES - 1)
    here = src[pl.ds(start, count), :]
    before = src[pl.ds(start - 1, count), :]
    return pltpu.roll(jnp.where(lanes(count) < LANES - turn, here, before), turn, axis=1)


def local_levels(first, mid, low, high, lag, out, width):
    src, dst = first, mid
    for level in range(1, LOCAL):
        span = 2 ** (level + 1)
        target = out if level == LOCAL - 1 else dst
        for row in range(ROWS):
            start = row - row % span
            low_at = GUARD + (start + low[level, row]) * width
            high_at = GUARD + (start + span // 2 + high[level, row]) * width
            for chunk in range(0, width, 8):
                target[pl.ds(GUARD + row * width + chunk, 8), :] = src[
                    pl.ds(low_at + chunk, 8), :
                ] + delayed(src, high_at + chunk, lag[level, row], 8)
        src, dst = dst, src


def first_level(pair_low, pair_high, buf, row, width):
    before = jnp.concatenate([jnp.zeros((1, LANES), F32), pair_high[: width - 1]], axis=0)
    late = pltpu.roll(jnp.where(lanes(width) < LANES - 1, pair_high, before), 1, axis=1)
    buf[pl.ds(GUARD + row * width, width), :] = pair_low + pair_high
    buf[pl.ds(GUARD + (row + 1) * width, width), :] = pair_low + late


def main_kernel(x, low, high, lag, low_v, high_v, lag_v, out, head, tab, buf_a, buf_b):
    zeros = jnp.zeros((GUARD, LANES), F32)
    for buf in (buf_a, buf_b, out):
        buf[0:GUARD, :] = zeros
    for group in range(8):
        head[pl.ds(group * 32, 32), :] = x[pl.ds(group * 128, 32), :]
    for at, table in enumerate((low_v, high_v, lag_v)):
        tab[pl.ds(2 * at, 2), :] = table[LOCAL + 1 : LEVELS, :]
    tab[6:8, :] = jnp.zeros((2, ROWS), jnp.int32)
    for row in range(0, ROWS, 2):
        at = (row // 8) * 128 + row % 8
        first_level(
            x[pl.ds(at, CHUNKS, stride=8), :],
            x[pl.ds(at + 1, CHUNKS, stride=8), :],
            buf_a,
            row,
            CHUNKS,
        )
    local_levels(buf_a, buf_b, low, high, lag, out, CHUNKS)


def head_kernel(halo, head, low, high, lag, out, buf_a, buf_b):
    zeros = jnp.zeros((GUARD, LANES), F32)
    for buf in (buf_a, buf_b, out):
        buf[0:GUARD, :] = zeros
    for row in range(0, ROWS, 2):
        at = (row // 8) * 32 + row % 8
        pair = [
            jnp.concatenate(
                [halo[pl.ds(at + k, 4, stride=8), :], head[pl.ds(at + k, 4, stride=8), :]], axis=0
            )
            for k in range(2)
        ]
        first_level(*pair, buf_a, row, 8)
    local_levels(buf_a, buf_b, low, high, lag, out, 8)


def cross_level(low_src, high_src, low, high, lag, width, put):
    for row in range(ROWS):
        low_at = GUARD + low[LOCAL, row] * width
        high_at = GUARD + high[LOCAL, row] * width
        for chunk in range(0, width, 8):
            put(
                row,
                chunk,
                low_src[pl.ds(low_at + chunk, 8), :]
                + delayed(high_src, high_at + chunk, lag[LOCAL, row], 8),
            )


def on_core(own, partner, run):
    core = jnp.bitwise_and(lax.axis_index("freq"), 1)
    pl.when(core == 0)(lambda: run(own, partner))
    pl.when(core == 1)(lambda: run(partner, own))


def core_main_kernel(own, partner, low, high, lag, out):
    def put(row, chunk, value):
        out[pl.ds(row * CHUNKS + chunk, 8), :] = value

    on_core(own, partner, lambda a, b: cross_level(a, b, low, high, lag, CHUNKS, put))


def core_head_kernel(own, partner, main, low, high, lag, out):
    width = HALO + CHUNKS

    def put(row, chunk, value):
        out[pl.ds(row * width, 8), :] = value

    on_core(own, partner, lambda a, b: cross_level(a, b, low, high, lag, 8, put))
    for row in range(ROWS):
        for chunk in (4, 8, 12):
            out[pl.ds(row * width + HALO + chunk, 4), :] = main[pl.ds(row * CHUNKS + chunk, 4), :]


def shares(l6, tabs, parts, outs):
    width = HALO + CHUNKS
    y = jnp.bitwise_and(lax.shift_right_logical(lax.axis_index("freq"), 1), 3)
    odd = jnp.bitwise_and(y, 1)
    upper7, upper8 = odd, lax.shift_right_logical(y, 1)
    own, across, near = tabs

    def table(k, entry, at):
        if k == 0:
            return own[entry, at]
        if k == 2:
            return across[entry, at]
        return near[entry + (0 if k == 1 else 8), at]

    for (steps, chunk, count), out in zip(parts, outs):

        def emit(k, steps=steps, chunk=chunk, count=count, out=out):
            for row in range(ROWS):
                via = table(k, 1 + 2 * upper8, row)
                lag = table(k, 5, row) * upper8
                source = table(k & 1, 2 * upper7, via)
                lag = lag + table(k & 1, 4, via) * upper7
                base = source * width + HALO + chunk
                for piece in range(0, count, 8):
                    out[pl.ds(row * count + piece, 8), :] = delayed(l6, base + piece, lag, 8)

        if steps in (0, 2):
            emit(steps)
        else:
            up = 1 if steps == 1 else 3
            pl.when(odd == 0)(lambda: emit(up))
            pl.when(odd == 1)(lambda: emit(4 - up))


def shares_kernel(parts, l6, own, across, near, *outs):
    shares(l6, (own, across, near), parts, outs)


def add_kernel(a, b, out):
    out[...] = a[...] + b[...]


def last_kernel(own, down_high, up_high, down_low, up_low, out):
    for row in range(ROWS):
        at = (row // 8) * 128 + row % 8
        for half, (a, b) in enumerate(((down_low, up_low), (down_high, up_high))):
            value = (
                own[pl.ds(row * CHUNKS + 8 * half, 8), :]
                + a[pl.ds(row * 8, 8), :]
                + b[pl.ds(row * 8, 8), :]
            )
            out[pl.ds(at + 64 * half, 8, stride=8), :] = value * SCALE


def call(kernel, ins, outs, scratch=()):
    values = [in_vmem(a) if where == "v" else a for a, where in ins]
    specs = [smem_spec() if where == "s" else vmem_spec() for _, where in ins]
    return pl.pallas_call(
        kernel,
        out_shape=outs,
        in_specs=specs,
        out_specs=[vmem_spec()] * len(outs),
        scratch_shapes=list(scratch),
    )(*values)


def pinned(sublanes, lane_count=LANES, dtype=F32):
    return pltpu.VMEM((sublanes, lane_count), dtype)


def ring(steps):
    return [(i, (i & ~6) | ((((i >> 1) + steps) & 3) << 1)) for i in range(64)]


def swap(bit):
    return [(i, i ^ bit) for i in range(64)]


def on_device(x, low, high, lag):
    tiles = x.reshape(8, 8, CHUNKS, LANES).transpose(0, 2, 1, 3)
    tail = tiles[:, CHUNKS - HALO :].reshape(8 * HALO * 8, LANES)
    halo = lax.ppermute(tail, "tm", [(0, 1), (1, 2), (2, 3)])
    tables = [(low, "s"), (high, "s"), (lag, "s")]

    l5, head, own_tab = call(
        main_kernel,
        [(tiles.reshape(1024, LANES), "b"), *tables, (low, "b"), (high, "b"), (lag, "b")],
        [pinned(GUARD + 1024), pinned(256), pinned(8, ROWS, jnp.int32)],
        [pltpu.VMEM((GUARD + 1024, LANES), F32)] * 2,
    )
    l5_far = lax.ppermute(l5, "freq", swap(1))
    across = lax.ppermute(own_tab, "freq", swap(4))
    near = lax.ppermute(jnp.concatenate([own_tab, across], axis=0), "freq", swap(2))
    (l5h,) = call(
        head_kernel,
        [(halo, "v"), (head, "v"), *tables],
        [pinned(GUARD + 512)],
        [pltpu.VMEM((GUARD + 512, LANES), F32)] * 2,
    )
    l5h_far = lax.ppermute(l5h, "freq", swap(1))
    (l6m,) = call(core_main_kernel, [(l5, "v"), (l5_far, "v"), *tables], [pinned(1024)])
    (l6,) = call(
        core_head_kernel,
        [(l5h, "v"), (l5h_far, "v"), (l6m, "v"), *tables],
        [pinned(ROWS * (HALO + CHUNKS))],
    )
    tabs = [(own_tab, "s"), (across, "s"), (near, "s")]

    def share(*parts):
        return call(
            functools.partial(shares_kernel, parts),
            [(l6, "v"), *tabs],
            [pinned(ROWS * count) for _, _, count in parts],
        )

    def add(a, b):
        return call(add_kernel, [(a, "v"), (b, "v")], [pinned(a.shape[0])])[0]

    one_up, one_down = ring(1), ring(-1)
    far_up, far_down = share((2, 8, 8), (2, 0, 8))
    relay_up = lax.ppermute(far_up, "freq", one_up)
    relay_down = lax.ppermute(far_down, "freq", one_down)
    next_up, next_down = share((1, 0, 8), (3, 8, 8))
    low_up = lax.ppermute(next_up, "freq", one_up)
    high_down = lax.ppermute(next_down, "freq", one_down)
    more_up, more_down, mine = share((1, 8, 8), (3, 0, 8), (0, 0, 16))
    high_up = lax.ppermute(add(more_up, relay_up), "freq", one_up)
    low_down = lax.ppermute(add(more_down, relay_down), "freq", one_down)
    (out,) = call(
        last_kernel,
        [(mine, "v"), (high_down, "v"), (high_up, "v"), (low_down, "v"), (low_up, "v")],
        [jax.ShapeDtypeStruct((1024, LANES), F32)],
    )
    return out.reshape(8, CHUNKS, 8, LANES).transpose(0, 2, 1, 3).reshape(ROWS, CHUNKS * LANES)


def solution(mesh):
    placed = (P("freq", "tm"), P(None, "freq"), P(None, "freq"), P(None, "freq"))
    return jax.shard_map(
        on_device, mesh=mesh, in_specs=placed, out_specs=P("freq", "tm"), check_vma=False
    )
```

```python
import functools
import math

import jax
import jax.numpy as jnp
from jax import lax
from jax.experimental import pallas as pl
from jax.experimental.pallas import tpu as pltpu
from jax.sharding import PartitionSpec as P

LOCAL = 6
LEVELS = 9
ROWS = 64
LANES = 128
CHUNKS = 16
PITCH = 24
PACKED = 18
REACH = 9
SCALE = 1.0 / math.sqrt(2.0**LEVELS)
F32 = jnp.float32
HEAD = ((2, 0, 4), (1, 0, 4), (3, 0, 4), (0, 0, 4))


def lanes(count):
    return lax.broadcasted_iota(jnp.int32, (count, LANES), 1)


def place():
    at = lax.axis_index("freq")
    return [jnp.bitwise_and(lax.shift_right_logical(at, bit), 1) for bit in range(3)]


def turned(here, before, turn):
    return pltpu.roll(
        jnp.where(lanes(here.shape[0]) < LANES - turn, here, before), turn, axis=1
    )


def level_codes(low, high, lag):
    row = lax.broadcasted_iota(jnp.int32, (LEVELS, ROWS), 1)
    level = lax.broadcasted_iota(jnp.int32, (LEVELS, ROWS), 0)
    span = lax.shift_left(2, level)
    local = level < LOCAL
    start = jnp.where(local, jnp.bitwise_and(row, -span), 0)
    half = jnp.where(local, lax.shift_right_logical(span, 1), 0)
    pitch = jnp.where(local, PITCH, PACKED)
    return (start + low) * pitch + (start + half + high) * pitch * 2048 + lag * 2**22


def opened(code):
    return (
        jnp.bitwise_and(code, 2047),
        jnp.bitwise_and(lax.shift_right_logical(code, 11), 2047),
        lax.shift_right_logical(code, 22),
    )


def pieces(src, code, skip, high_skip, spans):
    low_at, high_at, turn = opened(code)
    return [
        src[pl.ds(low_at + (skip + first), count), :]
        + turned(
            src[pl.ds(high_at + (high_skip + first), count), :],
            src[pl.ds(high_at + (high_skip + first - 1), count), :],
            turn,
        )
        for first, count in spans
    ]


WHOLE = ((0, 8), (8, 8), (16, 1))


def main_kernel(
    x_h, low_h, high_h, lag_h, out, tab, codes, x, low, high, lag, plan, buf_a, buf_b, sems
):
    copies = [
        pltpu.make_async_copy(source, target, sems.at[at])
        for at, (source, target) in enumerate(((low_h, low), (high_h, high), (lag_h, lag)))
    ]
    parts = [
        pltpu.make_async_copy(
            x_h.at[pl.ds(part * 256, 256)], x.at[pl.ds(part * 256, 256)], sems.at[3 + part]
        )
        for part in range(4)
    ]
    for copy in copies + parts:
        copy.start()
    for row in range(ROWS):
        out[pl.ds(row * PACKED, 1), :] = jnp.zeros((1, LANES), F32)
    for row in range(ROWS + 1):
        for buf in (buf_a, buf_b):
            buf[pl.ds(row * PITCH, 8), :] = jnp.zeros((8, LANES), F32)
    for copy in copies:
        copy.wait()
    plan[...] = jnp.zeros_like(plan)
    plan[0:LEVELS, 0:ROWS] = level_codes(low[...], high[...], lag[...])
    planned = pltpu.make_async_copy(plan, codes, sems.at[7])
    planned.start()
    tab[...] = jnp.zeros_like(tab)
    for at, table in enumerate((low, high, lag)):
        tab[pl.ds(2 * at, 2), 0:ROWS] = table[LOCAL + 1 : LEVELS, :]
    none = jnp.zeros((1, LANES), F32)
    for part, copy in enumerate(parts):
        copy.wait()
        for row in range(part * 16, part * 16 + 16, 2):
            at = (row // 8) * 128 + row % 8
            low_row = x[pl.ds(at, CHUNKS, stride=8), :]
            high_row = x[pl.ds(at + 1, CHUNKS, stride=8), :]
            before = jnp.concatenate([none, high_row[: CHUNKS - 1]], axis=0)
            to = row * PITCH + 8
            buf_a[pl.ds(to, CHUNKS), :] = low_row + high_row
            buf_a[pl.ds(to + PITCH, CHUNKS), :] = low_row + turned(high_row, before, 1)
            buf_a[pl.ds(to + PITCH + CHUNKS, 1), :] = turned(none, high_row[CHUNKS - 1 :], 1)
    planned.wait()
    src, dst = buf_a, buf_b
    for level in range(1, LOCAL):
        last = level == LOCAL - 1
        for row in range(ROWS):
            to = row * PACKED + 1 if last else row * PITCH + 8
            for (first, count), piece in zip(WHOLE, pieces(src, codes[level, row], 8, 8, WHOLE)):
                (out if last else dst)[pl.ds(to + first, count), :] = piece
        src, dst = dst, src


def term_codes(tab7, tab8, odd, upper, pitch):
    def rows(tab, at):
        return jnp.broadcast_to(tab[at : at + 1, :], (8, LANES))

    via = jnp.where(upper == 1, rows(tab8, 3), rows(tab8, 1))
    late = jnp.where(upper == 1, rows(tab8, 5), 0)
    source = jnp.where(odd == 1, rows(tab7, 2), rows(tab7, 0))
    later = jnp.where(odd == 1, rows(tab7, 4), 0)
    late = late + jnp.take_along_axis(later, via, axis=1)
    source = jnp.take_along_axis(source, via, axis=1)
    at = source * pitch - lax.shift_right_logical(late, 7)
    return (at * LANES + jnp.bitwise_and(late, LANES - 1))[0:1]


def shares(src, ahead, codes, parts, put, narrow=False):
    for part, (which, chunk, count) in enumerate(parts):
        for row in range(ROWS):
            code = codes[which, row]
            at = lax.shift_right_arithmetic(code, 7)
            if narrow:
                at = at - lax.shift_left(lax.shift_right_arithmetic(at + 8, 4), 3)
            turn = jnp.bitwise_and(code, LANES - 1)
            for first in range(0, count, 8):
                size = min(8, count - first)
                to = ahead + chunk + first
                put(
                    part,
                    row * count + first,
                    size,
                    turned(src[pl.ds(at + to, size), :], src[pl.ds(at + (to - 1), size), :], turn),
                )


def into(*outs):
    def put(part, at, size, value):
        outs[part][pl.ds(at, size), :] = value

    return put


def core_main_kernel(
    own, partner, codes, tab, l6, long_up, long_down, short_up, short_down, edge, both
):
    core = place()[0]
    size = own.shape[0]
    both[pl.ds(pl.multiple_of(core * size, 8), size), :] = own[...]
    both[pl.ds(pl.multiple_of((1 - core) * size, 8), size), :] = partner[...]
    for message in (long_up, long_down):
        message[0:8, :] = tab[...].astype(F32)
    for row in range(ROWS):
        first, second, past = pieces(both, codes[LOCAL, row], 1, size + 1, WHOLE)
        l6[pl.ds(row * CHUNKS, 8), :] = first
        l6[pl.ds(row * CHUNKS + 8, 8), :] = second
        edge[pl.ds(row * 4, 3), :] = second[5:8]
        edge[pl.ds(row * 4 + 3, 1), :] = past
        at = 8 + row * REACH
        long_up[pl.ds(at, 1), :] = first[7:8]
        long_up[pl.ds(at + 1, 8), :] = second
        long_down[pl.ds(at, 7), :] = first[1:8]
        long_down[pl.ds(at + 7, 2), :] = second[0:2]
        short_up[pl.ds(row * 6, 6), :] = first[1:7]
        short_down[pl.ds(row * 6, 6), :] = second[2:8]


def tables_of(message):
    return message[0:8, :].astype(jnp.int32)


def relay_kernel(long_up, long_down, up, down, plan, terms, sem):
    _, odd, upper = place()
    below, above = tables_of(long_up), tables_of(long_down)
    same = jnp.bitwise_xor(upper, odd)
    plan[...] = jnp.zeros_like(plan)
    plan[0:1, :] = term_codes(below, above, 1 - odd, 1 - same, REACH)
    plan[1:2, :] = term_codes(above, below, 1 - odd, same, REACH)
    copy = pltpu.make_async_copy(plan, terms, sem)
    copy.start()
    copy.wait()
    shares(long_up, 11, terms, ((0, 0, 6),), into(up))
    shares(long_down, 11, terms, ((1, 0, 6),), into(down))


def head_kernel(
    l6, edge, tab, across, long_up, long_down, far, up, down, mine, terms, buf, plan, sem
):
    _, odd, upper = place()
    own, other = tab[...], across[...]
    below, above = tables_of(long_up), tables_of(long_down)
    pair = jnp.where(odd == 1, below, above)
    plan[...] = jnp.zeros_like(plan)
    plan[0:1, :] = term_codes(own, own, odd, upper, CHUNKS)
    plan[1:2, :] = term_codes(pair, above, odd, upper, CHUNKS)
    plan[2:3, :] = term_codes(own, other, odd, upper, CHUNKS)
    plan[3:4, :] = term_codes(pair, below, odd, upper, CHUNKS)
    near = term_codes(own, own, 1 - odd, upper, CHUNKS)
    away = term_codes(other, own, 1 - odd, 1 - upper, CHUNKS)
    plan[4:5, :] = jnp.where(odd == 1, near, away)
    plan[5:6, :] = jnp.where(odd == 1, away, near)
    copy = pltpu.make_async_copy(plan, terms, sem)
    copy.start()
    inner = lax.axis_index("tm") > 0
    for row in range(ROWS):
        ahead = jnp.where(inner, edge[pl.ds(row * 4, 4), :], 0.0)
        buf[pl.ds(row * 8 + 1, 3), :] = ahead[0:3]
        buf[pl.ds(row * 8 + 4, 1), :] = ahead[3:4] + l6[pl.ds(row * CHUNKS, 1), :]
        buf[pl.ds(row * 8 + 5, 3), :] = l6[pl.ds(row * CHUNKS + 1, 3), :]
    copy.wait()
    shares(buf, 4, terms, HEAD, into(far, up, down, mine), narrow=True)


def direct_kernel(l6, long_up, long_down, short_up, short_down, terms, out, low_buf, high_buf):
    for row in range(ROWS):
        at, to = 8 + row * REACH, row * CHUNKS
        low_buf[pl.ds(to + 1, 6), :] = short_up[pl.ds(row * 6, 6), :]
        low_buf[pl.ds(to + 7, 9), :] = long_up[pl.ds(at, 9), :]
        high_buf[pl.ds(to + 1, 9), :] = long_down[pl.ds(at, 9), :]
        high_buf[pl.ds(to + 10, 6), :] = short_down[pl.ds(row * 6, 6), :]
    for row in range(ROWS):
        for first, count in ((4, 8), (12, 4)):
            total = None
            for which, src in ((0, l6), (4, low_buf), (5, high_buf)):
                code = terms[which, row]
                at = lax.shift_right_arithmetic(code, 7)
                term = turned(
                    src[pl.ds(at + first, count), :],
                    src[pl.ds(at + (first - 1), count), :],
                    jnp.bitwise_and(code, LANES - 1),
                )
                total = term if total is None else total + term
            out[pl.ds(row * 12 + first - 4, count), :] = total


def last_kernel(mine, mid_down, high_up, mine_head, far, up, down, out):
    for row in range(ROWS):
        at = (row // 8) * 128 + row % 8
        head = [a[pl.ds(row * 4, 4), :] for a in (mine_head, far, up, down)]
        out[pl.ds(at, 4, stride=8), :] = (head[0] + head[1] + head[2] + head[3]) * SCALE
        for chunk, arrived in ((4, mid_down), (10, high_up)):
            value = mine[pl.ds(row * 12 + chunk - 4, 6), :] + arrived[pl.ds(row * 6, 6), :]
            out[pl.ds(at + 8 * chunk, 6, stride=8), :] = value * SCALE


def call(kernel, ins, outs, scratch=()):
    pins = {"v": pltpu.VMEM, "t": pltpu.SMEM, "h": pltpu.HBM}
    kinds = {"v": pltpu.VMEM, "t": pltpu.SMEM, "h": pltpu.HBM}
    values = [
        pltpu.with_memory_space_constraint(a, pins[where]) if where in pins else a for a, where in ins
    ]
    return pl.pallas_call(
        kernel,
        out_shape=outs,
        in_specs=[pl.BlockSpec(memory_space=kinds[where]) for _, where in ins],
        out_specs=[
            pl.BlockSpec(memory_space=pltpu.SMEM if "smem" in str(o).lower() else pltpu.VMEM) for o in outs
        ],
        scratch_shapes=list(scratch),
        compiler_params=pltpu.CompilerParams(vmem_limit_bytes=16 * 2**20),
    )(*values)


def pinned(sublanes, lane_count=LANES, dtype=F32):
    return pltpu.VMEM((sublanes, lane_count), dtype)


def ring(steps):
    return [(i, (i & ~6) | ((((i >> 1) + steps) & 3) << 1)) for i in range(64)]


def swap(bit):
    return [(i, i ^ bit) for i in range(64)]


def on_device(x, low, high, lag):
    tiles = x.reshape(8, 8, CHUNKS, LANES).transpose(0, 2, 1, 3).reshape(1024, LANES)
    sem = pltpu.SemaphoreType.DMA
    ints = jnp.int32
    one_up, one_down = ring(1), ring(-1)
    plan, terms_ref = pltpu.VMEM((8, LANES), ints), pltpu.SMEM((8, LANES), ints)

    l5, own_tab, codes = call(
        main_kernel,
        [(a, "h") for a in (tiles, low, high, lag)],
        [pinned(ROWS * PACKED), pinned(8, LANES, ints), pltpu.SMEM((16, LANES), ints)],
        [pltpu.VMEM((1024, LANES), F32)]
        + [pltpu.VMEM((LEVELS, ROWS), ints)] * 3
        + [pltpu.VMEM((16, LANES), ints)]
        + [pltpu.VMEM((ROWS * PITCH + 8, LANES), F32)] * 2
        + [sem((8,))],
    )
    l5_far = lax.ppermute(l5, "freq", swap(1))
    across = lax.ppermute(own_tab, "freq", swap(4))
    l6, long_up, long_down, short_up, short_down, edge = call(
        core_main_kernel,
        [(l5, "v"), (l5_far, "v"), (codes, "t"), (own_tab, "v")],
        [pinned(1024)]
        + [pinned(8 + ROWS * REACH)] * 2
        + [pinned(ROWS * 6)] * 2
        + [pinned(ROWS * 4)],
        [pltpu.VMEM((2 * ROWS * PACKED, LANES), F32)],
    )
    long_up = lax.ppermute(long_up, "freq", one_up)
    long_down = lax.ppermute(long_down, "freq", one_down)
    short_up = lax.ppermute(short_up, "freq", one_up)
    short_down = lax.ppermute(short_down, "freq", one_down)
    edge = lax.ppermute(edge, "tm", [(i, (i + 1) % 4) for i in range(4)])

    relay_up, relay_down = call(
        relay_kernel,
        [(long_up, "v"), (long_down, "v")],
        [pinned(ROWS * 6), pinned(ROWS * 6)],
        [plan, terms_ref, sem],
    )
    high_up = lax.ppermute(relay_up, "freq", one_up)
    mid_down = lax.ppermute(relay_down, "freq", one_down)

    head_far, head_up, head_down, mine_head, terms = call(
        head_kernel,
        [(a, "v") for a in (l6, edge, own_tab, across, long_up, long_down)],
        [pinned(ROWS * 4)] * 4 + [terms_ref],
        [pltpu.VMEM((512, LANES), F32), plan, sem],
    )
    far = lax.ppermute(head_far, "freq", swap(4))
    up = lax.ppermute(head_up, "freq", one_up)
    down = lax.ppermute(head_down, "freq", one_down)
    (mine,) = call(
        direct_kernel,
        [(a, "v") for a in (l6, long_up, long_down, short_up, short_down)] + [(terms, "t")],
        [pinned(ROWS * 12)],
        [pltpu.VMEM((1024, LANES), F32)] * 2,
    )
    last = [mine, mid_down, high_up, mine_head, far, up, down]
    (out,) = call(
        last_kernel, [(a, "v") for a in last], [jax.ShapeDtypeStruct((1024, LANES), F32)]
    )
    return out.reshape(8, CHUNKS, 8, LANES).transpose(0, 2, 1, 3).reshape(ROWS, CHUNKS * LANES)


def solution(mesh):
    placed = (P("freq", "tm"), P(None, "freq"), P(None, "freq"), P(None, "freq"))
    return jax.shard_map(
        on_device, mesh=mesh, in_specs=placed, out_specs=P("freq", "tm"), check_vma=False
    )
```

```python
import functools
import math

import jax
import jax.numpy as jnp
from jax import lax
from jax.experimental import pallas as pl
from jax.experimental.pallas import tpu as pltpu
from jax.sharding import PartitionSpec as P

LOCAL = 6
LEVELS = 9
ROWS = 64
LANES = 128
CHUNKS = 16
PITCH = 24
PACKED = 18
WIDE = 20
PART = 10
SPARE = 3
UP, DOWN = 19 - PART + SPARE, PART - 1 + SPARE
REST_UP, REST_DOWN = PART - SPARE, 20 - PART - SPARE
SCALE = 1.0 / math.sqrt(2.0**LEVELS)
F32 = jnp.float32


def lanes(count):
    return lax.broadcasted_iota(jnp.int32, (count, LANES), 1)


def place():
    at = lax.axis_index("freq")
    return [jnp.bitwise_and(lax.shift_right_logical(at, bit), 1) for bit in range(3)]


def turned(here, before, turn):
    return pltpu.roll(
        jnp.where(lanes(here.shape[0]) < LANES - turn, here, before), turn, axis=1
    )


def level_codes(low, high, lag):
    row = lax.broadcasted_iota(jnp.int32, (LEVELS, ROWS), 1)
    level = lax.broadcasted_iota(jnp.int32, (LEVELS, ROWS), 0)
    span = lax.shift_left(2, level)
    local = level < LOCAL
    start = jnp.where(local, jnp.bitwise_and(row, -span), 0)
    half = jnp.where(local, lax.shift_right_logical(span, 1), 0)
    pitch = jnp.where(local, PITCH, PACKED)
    return (start + low) * pitch + (start + half + high) * pitch * 2048 + lag * 2**22


def opened(code):
    return (
        jnp.bitwise_and(code, 2047),
        jnp.bitwise_and(lax.shift_right_logical(code, 11), 2047),
        lax.shift_right_logical(code, 22),
    )


def pieces(src, code, skip, high_skip, spans):
    low_at, high_at, turn = opened(code)
    return [
        src[pl.ds(low_at + (skip + first), count), :]
        + turned(
            src[pl.ds(high_at + (high_skip + first), count), :],
            src[pl.ds(high_at + (high_skip + first - 1), count), :],
            turn,
        )
        for first, count in spans
    ]


WHOLE = ((0, 8), (8, 8), (16, 1))


def main_kernel(
    x_h, low_h, high_h, lag_h, out, tab, codes, x, low, high, lag, plan, buf_a, buf_b, sems
):
    copies = [
        pltpu.make_async_copy(source, target, sems.at[at])
        for at, (source, target) in enumerate(((low_h, low), (high_h, high), (lag_h, lag)))
    ]
    parts = [
        pltpu.make_async_copy(
            x_h.at[pl.ds(part * 256, 256)], x.at[pl.ds(part * 256, 256)], sems.at[3 + part]
        )
        for part in range(4)
    ]
    for copy in copies + parts:
        copy.start()
    for row in range(ROWS):
        out[pl.ds(row * PACKED, 1), :] = jnp.zeros((1, LANES), F32)
    for row in range(ROWS + 1):
        for buf in (buf_a, buf_b):
            buf[pl.ds(row * PITCH, 8), :] = jnp.zeros((8, LANES), F32)
    for copy in copies:
        copy.wait()
    plan[...] = jnp.zeros_like(plan)
    plan[0:LEVELS, 0:ROWS] = level_codes(low[...], high[...], lag[...])
    planned = pltpu.make_async_copy(plan, codes, sems.at[7])
    planned.start()
    tab[...] = jnp.zeros_like(tab)
    for at, table in enumerate((low, high, lag)):
        tab[pl.ds(2 * at, 2), 0:ROWS] = table[LOCAL + 1 : LEVELS, :]
    none = jnp.zeros((1, LANES), F32)
    for part, copy in enumerate(parts):
        copy.wait()
        for row in range(part * 16, part * 16 + 16, 2):
            at = (row // 8) * 128 + row % 8
            low_row = x[pl.ds(at, CHUNKS, stride=8), :]
            high_row = x[pl.ds(at + 1, CHUNKS, stride=8), :]
            before = jnp.concatenate([none, high_row[: CHUNKS - 1]], axis=0)
            to = row * PITCH + 8
            buf_a[pl.ds(to, CHUNKS), :] = low_row + high_row
            buf_a[pl.ds(to + PITCH, CHUNKS), :] = low_row + turned(high_row, before, 1)
            buf_a[pl.ds(to + PITCH + CHUNKS, 1), :] = turned(none, high_row[CHUNKS - 1 :], 1)
    planned.wait()
    src, dst = buf_a, buf_b
    for level in range(1, LOCAL):
        last = level == LOCAL - 1
        for row in range(ROWS):
            to = row * PACKED + 1 if last else row * PITCH + 8
            for (first, count), piece in zip(WHOLE, pieces(src, codes[level, row], 8, 8, WHOLE)):
                (out if last else dst)[pl.ds(to + first, count), :] = piece
        src, dst = dst, src


def term_codes(tab7, tab8, odd, upper, pitch):
    def rows(tab, at):
        return jnp.broadcast_to(tab[at : at + 1, :], (8, LANES))

    via = jnp.where(upper == 1, rows(tab8, 3), rows(tab8, 1))
    late = jnp.where(upper == 1, rows(tab8, 5), 0)
    source = jnp.where(odd == 1, rows(tab7, 2), rows(tab7, 0))
    later = jnp.where(odd == 1, rows(tab7, 4), 0)
    late = late + jnp.take_along_axis(later, via, axis=1)
    source = jnp.take_along_axis(source, via, axis=1)
    at = source * pitch - lax.shift_right_logical(late, 7)
    return (at * LANES + jnp.bitwise_and(late, LANES - 1))[0:1]


def shares(src, ahead, codes, which, count, put):
    for row in range(ROWS):
        code = codes[which, row]
        at = lax.shift_right_arithmetic(code, 7)
        turn = jnp.bitwise_and(code, LANES - 1)
        for first in range(0, count, 8):
            size = min(8, count - first)
            to = ahead + first
            value = turned(
                src[pl.ds(at + to, size), :], src[pl.ds(at + (to - 1), size), :], turn
            )
            put(row * count + first, size, value)


def into(out):
    def put(at, size, value):
        out[pl.ds(at, size), :] = value

    return put


def core_main_kernel(own, partner, codes, tab, l6, long_up, long_down, edge, both):
    core = place()[0]
    size = own.shape[0]
    both[pl.ds(pl.multiple_of(core * size, 8), size), :] = own[...]
    both[pl.ds(pl.multiple_of((1 - core) * size, 8), size), :] = partner[...]
    for message in (long_up, long_down):
        message[0:8, :] = tab[...].astype(F32)
    for row in range(ROWS):
        first, second, past = pieces(both, codes[LOCAL, row], 1, size + 1, WHOLE)
        l6[pl.ds(row * CHUNKS, 8), :] = first
        l6[pl.ds(row * CHUNKS + 8, 8), :] = second
        edge[pl.ds(row * 4, 3), :] = second[5:8]
        edge[pl.ds(row * 4 + 3, 1), :] = past
        at = 8 + row * UP
        long_up[pl.ds(at, UP - 8), :] = first[16 - UP :]
        long_up[pl.ds(at + UP - 8, 8), :] = second
        at = 8 + row * DOWN
        long_down[pl.ds(at, 7), :] = first[1:8]
        long_down[pl.ds(at + 7, DOWN - 7), :] = second[0 : DOWN - 7]


def history_kernel(l6, edge, whole, rest_up, rest_down):
    inner = lax.axis_index("tm") > 0
    for row in range(ROWS):
        at = row * WIDE
        ahead = jnp.where(inner, edge[pl.ds(row * 4, 4), :], 0.0)
        block = l6[pl.ds(row * CHUNKS, CHUNKS), :]
        whole[pl.ds(at, 1), :] = jnp.zeros((1, LANES), F32)
        whole[pl.ds(at + 1, 3), :] = ahead[0:3]
        whole[pl.ds(at + 4, 1), :] = ahead[3:4] + block[0:1]
        whole[pl.ds(at + 5, CHUNKS - 1), :] = block[1:]
        to = row * REST_UP
        rest_up[pl.ds(to, 3), :] = ahead[0:3]
        rest_up[pl.ds(to + 3, 1), :] = ahead[3:4] + block[0:1]
        rest_up[pl.ds(to + 4, REST_UP - 4), :] = block[1 : REST_UP - 3]
        to = row * REST_DOWN
        rest_down[pl.ds(to, 3), :] = ahead[0:3]
        rest_down[pl.ds(to + 3, 1), :] = ahead[3:4] + block[0:1]
        rest_down[pl.ds(to + 4, REST_DOWN - 4), :] = block[20 - REST_DOWN :]


def relay_kernel(long_up, long_down, up, down, terms, plan, sem):
    _, odd, upper = place()
    below, above = [message[0:8, :].astype(jnp.int32) for message in (long_up, long_down)]
    same = jnp.bitwise_xor(upper, odd)
    plan[...] = jnp.zeros_like(plan)
    plan[0:1, :] = term_codes(below, above, 1 - odd, 1 - same, UP)
    plan[1:2, :] = term_codes(above, below, 1 - odd, same, DOWN)
    plan[2:3, :] = term_codes(below, above, 1 - odd, 1 - same, REST_UP)
    plan[3:4, :] = term_codes(above, below, 1 - odd, same, 8)
    copy = pltpu.make_async_copy(plan, terms, sem)
    copy.start()
    up[ROWS * (16 - PART) :, :] = long_up[0:8, :]
    copy.wait()
    shares(long_up, 11 + SPARE, terms, 0, 16 - PART, into(up))
    shares(long_down, 11, terms, 1, PART - 4, into(down))


def first_relay_kernel(rest_up, rest_down, long_down, terms, tab, up, down, passed, buf):
    passed[...] = tab[...]
    shares(rest_up, 5, terms, 2, 2, into(up))
    for row in range(ROWS):
        buf[pl.ds(row * 8 + 1, 4), :] = rest_down[pl.ds(row * REST_DOWN, 4), :]
        buf[pl.ds(row * 8 + 5, 1), :] = long_down[pl.ds(8 + row * DOWN, 1), :]
    shares(buf, 4, terms, 3, 2, into(down))


def direct_kernel(
    whole, long_up, rest_up, long_down, rest_down, tab, relay, *refs
):
    out, low_buf, high_buf, plan, terms, sem = refs
    _, odd, upper = place()
    own, other = tab[...], relay[ROWS * (16 - PART) :, :].astype(jnp.int32)
    plan[...] = jnp.zeros_like(plan)
    plan[0:1, :] = term_codes(own, own, odd, upper, WIDE)
    near = term_codes(own, own, 1 - odd, upper, WIDE)
    away = term_codes(other, own, 1 - odd, 1 - upper, WIDE)
    plan[1:2, :] = jnp.where(odd == 1, near, away)
    plan[2:3, :] = jnp.where(odd == 1, away, near)
    copy = pltpu.make_async_copy(plan, terms, sem)
    copy.start()
    for row in range(ROWS):
        to, rest = row * WIDE, row * REST_DOWN
        low_buf[pl.ds(to + 1, REST_UP), :] = rest_up[pl.ds(row * REST_UP, REST_UP), :]
        low_buf[pl.ds(to + 1 + REST_UP, UP), :] = long_up[pl.ds(8 + row * UP, UP), :]
        high_buf[pl.ds(to + 1, 4), :] = rest_down[pl.ds(rest, 4), :]
        high_buf[pl.ds(to + 5, DOWN), :] = long_down[pl.ds(8 + row * DOWN, DOWN), :]
        high_buf[pl.ds(to + 5 + DOWN, REST_DOWN - 4), :] = rest_down[
            pl.ds(rest + 4, REST_DOWN - 4), :
        ]
    copy.wait()
    for row in range(ROWS):
        found = []
        for which in range(3):
            code = terms[which, row]
            found.append((lax.shift_right_arithmetic(code, 7), jnp.bitwise_and(code, LANES - 1)))
        for first in (0, 8):
            to = 4 + first
            total = None
            for src, (at, turn) in zip((whole, low_buf, high_buf), found):
                term = turned(src[pl.ds(at + to, 8), :], src[pl.ds(at + (to - 1), 8), :], turn)
                total = term if total is None else total + term
            out[pl.ds(row * CHUNKS + first, 8), :] = total


def last_kernel(mine, down_first, up_first, down, up, out):
    spans = ((down_first, 0, 2), (up_first, 2, 2), (down, 4, PART - 4), (up, PART, 16 - PART))
    for row in range(ROWS):
        at = (row // 8) * 128 + row % 8
        for arrived, chunk, count in spans:
            value = mine[pl.ds(row * CHUNKS + chunk, count), :] + arrived[pl.ds(row * count, count), :]
            out[pl.ds(at + 8 * chunk, count, stride=8), :] = value * SCALE


def call(kernel, ins, outs, scratch=()):
    pins = {"v": pltpu.VMEM, "t": pltpu.SMEM, "h": pltpu.HBM}
    kinds = {"v": pltpu.VMEM, "t": pltpu.SMEM, "h": pltpu.HBM}
    values = [
        pltpu.with_memory_space_constraint(a, pins[where]) if where in pins else a for a, where in ins
    ]
    return pl.pallas_call(
        kernel,
        out_shape=outs,
        in_specs=[pl.BlockSpec(memory_space=kinds[where]) for _, where in ins],
        out_specs=[
            pl.BlockSpec(memory_space=pltpu.SMEM if "smem" in str(o).lower() else pltpu.VMEM) for o in outs
        ],
        scratch_shapes=list(scratch),
        compiler_params=pltpu.CompilerParams(vmem_limit_bytes=16 * 2**20),
    )(*values)


def pinned(sublanes, lane_count=LANES, dtype=F32):
    return pltpu.VMEM((sublanes, lane_count), dtype)


def ring(steps):
    return [(i, (i & ~6) | ((((i >> 1) + steps) & 3) << 1)) for i in range(64)]


def swap(bit):
    return [(i, i ^ bit) for i in range(64)]


def on_device(x, low, high, lag):
    tiles = x.reshape(8, 8, CHUNKS, LANES).transpose(0, 2, 1, 3).reshape(1024, LANES)
    sem = pltpu.SemaphoreType.DMA
    ints = jnp.int32
    one_up, one_down = ring(1), ring(-1)
    plan, terms_ref = pltpu.VMEM((8, LANES), ints), pltpu.SMEM((8, LANES), ints)

    l5, own_tab, codes = call(
        main_kernel,
        [(a, "h") for a in (tiles, low, high, lag)],
        [pinned(ROWS * PACKED), pinned(8, LANES, ints), pltpu.SMEM((16, LANES), ints)],
        [pltpu.VMEM((1024, LANES), F32)]
        + [pltpu.VMEM((LEVELS, ROWS), ints)] * 3
        + [pltpu.VMEM((16, LANES), ints)]
        + [pltpu.VMEM((ROWS * PITCH + 8, LANES), F32)] * 2
        + [sem((8,))],
    )
    l5_far = lax.ppermute(l5, "freq", swap(1))
    l6, long_up, long_down, edge = call(
        core_main_kernel,
        [(l5, "v"), (l5_far, "v"), (codes, "t"), (own_tab, "v")],
        [pinned(1024), pinned(8 + ROWS * UP), pinned(8 + ROWS * DOWN), pinned(ROWS * 4)],
        [pltpu.VMEM((2 * ROWS * PACKED, LANES), F32)],
    )
    long_up = lax.ppermute(long_up, "freq", one_up)
    long_down = lax.ppermute(long_down, "freq", one_down)
    edge = lax.ppermute(edge, "tm", [(i, (i + 1) % 4) for i in range(4)])

    whole, rest_up, rest_down = call(
        history_kernel,
        [(l6, "v"), (edge, "v")],
        [pinned(ROWS * WIDE), pinned(ROWS * REST_UP), pinned(ROWS * REST_DOWN)],
    )
    rest_up = lax.ppermute(rest_up, "freq", one_up)
    rest_down = lax.ppermute(rest_down, "freq", one_down)

    relay_up, relay_down, terms = call(
        relay_kernel,
        [(long_up, "v"), (long_down, "v")],
        [pinned(ROWS * (16 - PART) + 8), pinned(ROWS * (PART - 4)), terms_ref],
        [plan, sem],
    )
    up = lax.ppermute(relay_up, "freq", one_up)
    down = lax.ppermute(relay_down, "freq", one_down)

    relay_up, relay_down, tab = call(
        first_relay_kernel,
        [(rest_up, "v"), (rest_down, "v"), (long_down, "v"), (terms, "t"), (own_tab, "v")],
        [pinned(ROWS * 2), pinned(ROWS * 2), pinned(8, LANES, ints)],
        [pltpu.VMEM((512, LANES), F32)],
    )
    up_first = lax.ppermute(relay_up, "freq", one_up)
    down_first = lax.ppermute(relay_down, "freq", one_down)

    (mine,) = call(
        direct_kernel,
        [(a, "v") for a in (whole, long_up, rest_up, long_down, rest_down, tab, up)],
        [pinned(ROWS * CHUNKS)],
        [pltpu.VMEM((ROWS * WIDE, LANES), F32)] * 2 + [plan, terms_ref, sem],
    )
    (out,) = call(
        last_kernel,
        [(a, "v") for a in (mine, down_first, up_first, down, up)],
        [jax.ShapeDtypeStruct((1024, LANES), F32)],
    )
    return out.reshape(8, CHUNKS, 8, LANES).transpose(0, 2, 1, 3).reshape(ROWS, CHUNKS * LANES)


def solution(mesh):
    placed = (P("freq", "tm"), P(None, "freq"), P(None, "freq"), P(None, "freq"))
    return jax.shard_map(
        on_device, mesh=mesh, in_specs=placed, out_specs=P("freq", "tm"), check_vma=False
    )
```

```python
import functools
import math

import jax
import jax.numpy as jnp
from jax import lax
from jax.experimental import pallas as pl
from jax.experimental.pallas import tpu as pltpu
from jax.sharding import PartitionSpec as P

LOCAL = 6
LEVELS = 9
ROWS = 64
LANES = 128
CHUNKS = 16
PITCH = 24
PACKED = 18
WIDE = 20
TO_PAIR, TO_CROSS = 12, 12
PAIR_REST, CROSS_REST = 19 - TO_PAIR, 19 - TO_CROSS
SCALE = 1.0 / math.sqrt(2.0**LEVELS)
F32 = jnp.float32


def lanes(count):
    return lax.broadcasted_iota(jnp.int32, (count, LANES), 1)


def place():
    at = lax.axis_index("freq")
    return [jnp.bitwise_and(lax.shift_right_logical(at, bit), 1) for bit in range(3)]


def turned(here, before, turn):
    return pltpu.roll(
        jnp.where(lanes(here.shape[0]) < LANES - turn, here, before), turn, axis=1
    )


def level_codes(low, high, lag):
    row = lax.broadcasted_iota(jnp.int32, (LEVELS, ROWS), 1)
    level = lax.broadcasted_iota(jnp.int32, (LEVELS, ROWS), 0)
    span = lax.shift_left(2, level)
    local = level < LOCAL
    start = jnp.where(local, jnp.bitwise_and(row, -span), 0)
    half = jnp.where(local, lax.shift_right_logical(span, 1), 0)
    pitch = jnp.where(local, PITCH, PACKED)
    return (start + low) * pitch + (start + half + high) * pitch * 2048 + lag * 2**22


def opened(code):
    return (
        jnp.bitwise_and(code, 2047),
        jnp.bitwise_and(lax.shift_right_logical(code, 11), 2047),
        lax.shift_right_logical(code, 22),
    )


def pieces(src, code, skip, high_skip, spans):
    low_at, high_at, turn = opened(code)
    return [
        src[pl.ds(low_at + (skip + first), count), :]
        + turned(
            src[pl.ds(high_at + (high_skip + first), count), :],
            src[pl.ds(high_at + (high_skip + first - 1), count), :],
            turn,
        )
        for first, count in spans
    ]


WHOLE = ((0, 8), (8, 8), (16, 1))


def main_kernel(
    x_h, low_h, high_h, lag_h, out, tab, codes, x, low, high, lag, plan, buf_a, buf_b, sems
):
    copies = [
        pltpu.make_async_copy(source, target, sems.at[at])
        for at, (source, target) in enumerate(((low_h, low), (high_h, high), (lag_h, lag)))
    ]
    parts = [
        pltpu.make_async_copy(
            x_h.at[pl.ds(part * 256, 256)], x.at[pl.ds(part * 256, 256)], sems.at[3 + part]
        )
        for part in range(4)
    ]
    for copy in copies + parts:
        copy.start()
    for row in range(ROWS):
        out[pl.ds(row * PACKED, 1), :] = jnp.zeros((1, LANES), F32)
    for row in range(ROWS + 1):
        for buf in (buf_a, buf_b):
            buf[pl.ds(row * PITCH, 8), :] = jnp.zeros((8, LANES), F32)
    for copy in copies:
        copy.wait()
    plan[...] = jnp.zeros_like(plan)
    plan[0:LEVELS, 0:ROWS] = level_codes(low[...], high[...], lag[...])
    planned = pltpu.make_async_copy(plan, codes, sems.at[7])
    planned.start()
    tab[...] = jnp.zeros_like(tab)
    for at, table in enumerate((low, high, lag)):
        tab[pl.ds(2 * at, 2), 0:ROWS] = table[LOCAL + 1 : LEVELS, :]
    none = jnp.zeros((1, LANES), F32)
    for part, copy in enumerate(parts):
        copy.wait()
        for row in range(part * 16, part * 16 + 16, 2):
            at = (row // 8) * 128 + row % 8
            low_row = x[pl.ds(at, CHUNKS, stride=8), :]
            high_row = x[pl.ds(at + 1, CHUNKS, stride=8), :]
            before = jnp.concatenate([none, high_row[: CHUNKS - 1]], axis=0)
            to = row * PITCH + 8
            buf_a[pl.ds(to, CHUNKS), :] = low_row + high_row
            buf_a[pl.ds(to + PITCH, CHUNKS), :] = low_row + turned(high_row, before, 1)
            buf_a[pl.ds(to + PITCH + CHUNKS, 1), :] = turned(none, high_row[CHUNKS - 1 :], 1)
    planned.wait()
    src, dst = buf_a, buf_b
    for level in range(1, LOCAL):
        last = level == LOCAL - 1
        for row in range(ROWS):
            to = row * PACKED + 1 if last else row * PITCH + 8
            for (first, count), piece in zip(WHOLE, pieces(src, codes[level, row], 8, 8, WHOLE)):
                (out if last else dst)[pl.ds(to + first, count), :] = piece
        src, dst = dst, src


def term_codes(tab7, tab8, odd, upper, pitch):
    def rows(tab, at):
        return jnp.broadcast_to(tab[at : at + 1, :], (8, LANES))

    via = jnp.where(upper == 1, rows(tab8, 3), rows(tab8, 1))
    late = jnp.where(upper == 1, rows(tab8, 5), 0)
    source = jnp.where(odd == 1, rows(tab7, 2), rows(tab7, 0))
    later = jnp.where(odd == 1, rows(tab7, 4), 0)
    late = late + jnp.take_along_axis(later, via, axis=1)
    source = jnp.take_along_axis(source, via, axis=1)
    at = source * pitch - lax.shift_right_logical(late, 7)
    return (at * LANES + jnp.bitwise_and(late, LANES - 1))[0:1]


def shares(src, ahead, codes, which, count, put):
    for row in range(ROWS):
        code = codes[which, row]
        at = lax.shift_right_arithmetic(code, 7)
        turn = jnp.bitwise_and(code, LANES - 1)
        for first in range(0, count, 8):
            size = min(8, count - first)
            to = ahead + first
            value = turned(
                src[pl.ds(at + to, size), :], src[pl.ds(at + (to - 1), size), :], turn
            )
            put(row * count + first, size, value)


def into(out):
    def put(at, size, value):
        out[pl.ds(at, size), :] = value

    return put


def core_main_kernel(own, partner, codes, tab, l6, to_pair, to_cross, edge, both):
    core = place()[0]
    size = own.shape[0]
    both[pl.ds(pl.multiple_of(core * size, 8), size), :] = own[...]
    both[pl.ds(pl.multiple_of((1 - core) * size, 8), size), :] = partner[...]
    for message in (to_pair, to_cross):
        message[0:8, :] = tab[...].astype(F32)
    for row in range(ROWS):
        first, second, past = pieces(both, codes[LOCAL, row], 1, size + 1, WHOLE)
        l6[pl.ds(row * CHUNKS, 8), :] = first
        l6[pl.ds(row * CHUNKS + 8, 8), :] = second
        edge[pl.ds(row * 4, 3), :] = second[5:8]
        edge[pl.ds(row * 4 + 3, 1), :] = past
        at = 8 + row * TO_PAIR
        to_pair[pl.ds(at, TO_PAIR - 8), :] = first[16 - TO_PAIR :]
        to_pair[pl.ds(at + TO_PAIR - 8, 8), :] = second
        at = 8 + row * TO_CROSS
        to_cross[pl.ds(at, 7), :] = first[1:8]
        to_cross[pl.ds(at + 7, TO_CROSS - 7), :] = second[0 : TO_CROSS - 7]


def history_kernel(l6, edge, whole, pair_rest, cross_rest):
    inner = lax.axis_index("tm") > 0
    for row in range(ROWS):
        at = row * WIDE
        ahead = jnp.where(inner, edge[pl.ds(row * 4, 4), :], 0.0)
        block = l6[pl.ds(row * CHUNKS, CHUNKS), :]
        whole[pl.ds(at, 1), :] = jnp.zeros((1, LANES), F32)
        whole[pl.ds(at + 1, 3), :] = ahead[0:3]
        whole[pl.ds(at + 4, 1), :] = ahead[3:4] + block[0:1]
        whole[pl.ds(at + 5, CHUNKS - 1), :] = block[1:]
        to = row * PAIR_REST
        pair_rest[pl.ds(to, 3), :] = ahead[0:3]
        pair_rest[pl.ds(to + 3, 1), :] = ahead[3:4] + block[0:1]
        pair_rest[pl.ds(to + 4, PAIR_REST - 4), :] = block[1 : PAIR_REST - 3]
        to = row * CROSS_REST
        cross_rest[pl.ds(to, 3), :] = ahead[0:3]
        cross_rest[pl.ds(to + 3, 1), :] = ahead[3:4] + block[0:1]
        cross_rest[pl.ds(to + 4, CROSS_REST - 4), :] = block[TO_CROSS + 1 :]


def tables_of(message):
    return message[0:8, :].astype(jnp.int32)


def relay_kernel(pair, cross, for_pair, for_cross, terms, plan, sem):
    _, odd, upper = place()
    pair_tab, cross_tab = tables_of(pair), tables_of(cross)
    plan[...] = jnp.zeros_like(plan)
    plan[0:1, :] = term_codes(cross_tab, pair_tab, 1 - odd, 1 - upper, TO_CROSS)
    plan[1:2, :] = term_codes(pair_tab, cross_tab, 1 - odd, upper, TO_PAIR)
    plan[2:3, :] = term_codes(cross_tab, pair_tab, 1 - odd, 1 - upper, 8)
    copy = pltpu.make_async_copy(plan, terms, sem)
    copy.start()
    for_pair[ROWS * 4 :, :] = cross[0:8, :]
    copy.wait()
    shares(cross, 8 + 3, terms, 0, 4, into(for_pair))
    shares(pair, 8 + TO_PAIR - 8, terms, 1, 8, into(for_cross))


def first_relay_kernel(pair, pair_rest, cross, cross_rest, terms, for_pair, pair_whole, buf):
    for row in range(ROWS):
        buf[pl.ds(row * 8 + 1, 4), :] = cross_rest[pl.ds(row * CROSS_REST, 4), :]
        buf[pl.ds(row * 8 + 5, 3), :] = cross[pl.ds(8 + row * TO_CROSS, 3), :]
    shares(buf, 4, terms, 2, 4, into(for_pair))
    for row in range(ROWS):
        to = row * WIDE
        pair_whole[pl.ds(to, 1), :] = jnp.zeros((1, LANES), F32)
        pair_whole[pl.ds(to + 1, PAIR_REST), :] = pair_rest[pl.ds(row * PAIR_REST, PAIR_REST), :]
        pair_whole[pl.ds(to + 1 + PAIR_REST, TO_PAIR), :] = pair[
            pl.ds(8 + row * TO_PAIR, TO_PAIR), :
        ]


def direct_kernel(whole, pair_whole, cross, cross_rest, tab, relay, out, buf, plan, terms, sem):
    _, odd, upper = place()
    own, other = tab[...], relay[ROWS * 4 :, :].astype(jnp.int32)
    plan[...] = jnp.zeros_like(plan)
    plan[0:1, :] = term_codes(own, own, odd, upper, WIDE)
    plan[1:2, :] = term_codes(own, own, 1 - odd, upper, WIDE)
    plan[2:3, :] = term_codes(other, own, 1 - odd, 1 - upper, WIDE)
    copy = pltpu.make_async_copy(plan, terms, sem)
    copy.start()
    for row in range(ROWS):
        to, rest = row * WIDE, row * CROSS_REST
        buf[pl.ds(to + 1, 4), :] = cross_rest[pl.ds(rest, 4), :]
        buf[pl.ds(to + 5, TO_CROSS), :] = cross[pl.ds(8 + row * TO_CROSS, TO_CROSS), :]
        buf[pl.ds(to + 5 + TO_CROSS, CROSS_REST - 4), :] = cross_rest[
            pl.ds(rest + 4, CROSS_REST - 4), :
        ]
    copy.wait()
    for row in range(ROWS):
        found = []
        for which in range(3):
            code = terms[which, row]
            found.append((lax.shift_right_arithmetic(code, 7), jnp.bitwise_and(code, LANES - 1)))
        for first in (0, 8):
            to = 4 + first
            total = None
            for src, (at, turn) in zip((whole, pair_whole, buf), found):
                term = turned(src[pl.ds(at + to, 8), :], src[pl.ds(at + (to - 1), 8), :], turn)
                total = term if total is None else total + term
            out[pl.ds(row * CHUNKS + first, 8), :] = total


def last_kernel(mine, first, second, rest, out):
    for row in range(ROWS):
        at = (row // 8) * 128 + row % 8
        for arrived, chunk, count in ((first, 0, 4), (second, 4, 4), (rest, 8, 8)):
            value = mine[pl.ds(row * CHUNKS + chunk, count), :] + arrived[pl.ds(row * count, count), :]
            out[pl.ds(at + 8 * chunk, count, stride=8), :] = value * SCALE


def call(kernel, ins, outs, scratch=()):
    pins = {"v": pltpu.VMEM, "t": pltpu.SMEM, "h": pltpu.HBM}
    kinds = {"v": pltpu.VMEM, "t": pltpu.SMEM, "h": pltpu.HBM}
    values = [
        pltpu.with_memory_space_constraint(a, pins[where]) if where in pins else a for a, where in ins
    ]
    return pl.pallas_call(
        kernel,
        out_shape=outs,
        in_specs=[pl.BlockSpec(memory_space=kinds[where]) for _, where in ins],
        out_specs=[
            pl.BlockSpec(memory_space=pltpu.SMEM if "smem" in str(o).lower() else pltpu.VMEM) for o in outs
        ],
        scratch_shapes=list(scratch),
        compiler_params=pltpu.CompilerParams(vmem_limit_bytes=16 * 2**20),
    )(*values)


def pinned(sublanes, lane_count=LANES, dtype=F32):
    return pltpu.VMEM((sublanes, lane_count), dtype)


def swap(bit):
    return [(i, i ^ bit) for i in range(64)]


def on_device(x, low, high, lag):
    tiles = x.reshape(8, 8, CHUNKS, LANES).transpose(0, 2, 1, 3).reshape(1024, LANES)
    sem = pltpu.SemaphoreType.DMA
    ints = jnp.int32
    by_pair, by_cross = swap(2), swap(6)
    plan, terms_ref = pltpu.VMEM((8, LANES), ints), pltpu.SMEM((8, LANES), ints)

    l5, own_tab, codes = call(
        main_kernel,
        [(a, "h") for a in (tiles, low, high, lag)],
        [pinned(ROWS * PACKED), pinned(8, LANES, ints), pltpu.SMEM((16, LANES), ints)],
        [pltpu.VMEM((1024, LANES), F32)]
        + [pltpu.VMEM((LEVELS, ROWS), ints)] * 3
        + [pltpu.VMEM((16, LANES), ints)]
        + [pltpu.VMEM((ROWS * PITCH + 8, LANES), F32)] * 2
        + [sem((8,))],
    )
    l5_far = lax.ppermute(l5, "freq", swap(1))
    l6, pair, cross, edge = call(
        core_main_kernel,
        [(l5, "v"), (l5_far, "v"), (codes, "t"), (own_tab, "v")],
        [pinned(1024), pinned(8 + ROWS * TO_PAIR), pinned(8 + ROWS * TO_CROSS), pinned(ROWS * 4)],
        [pltpu.VMEM((2 * ROWS * PACKED, LANES), F32)],
    )
    pair = lax.ppermute(pair, "freq", by_pair)
    cross = lax.ppermute(cross, "freq", by_cross)
    edge = lax.ppermute(edge, "tm", [(i, (i + 1) % 4) for i in range(4)])

    whole, pair_rest, cross_rest = call(
        history_kernel,
        [(l6, "v"), (edge, "v")],
        [pinned(ROWS * WIDE), pinned(ROWS * PAIR_REST), pinned(ROWS * CROSS_REST)],
    )
    pair_rest = lax.ppermute(pair_rest, "freq", by_pair)
    cross_rest = lax.ppermute(cross_rest, "freq", by_cross)

    for_pair, for_cross, terms = call(
        relay_kernel,
        [(pair, "v"), (cross, "v")],
        [pinned(ROWS * 4 + 8), pinned(ROWS * 8), terms_ref],
        [plan, sem],
    )
    second = lax.ppermute(for_pair, "freq", by_pair)
    rest = lax.ppermute(for_cross, "freq", by_cross)

    for_pair, pair_whole = call(
        first_relay_kernel,
        [(a, "v") for a in (pair, pair_rest, cross, cross_rest)] + [(terms, "t")],
        [pinned(ROWS * 4), pinned(ROWS * WIDE)],
        [pltpu.VMEM((512, LANES), F32)],
    )
    first = lax.ppermute(for_pair, "freq", by_pair)

    (mine,) = call(
        direct_kernel,
        [(a, "v") for a in (whole, pair_whole, cross, cross_rest, own_tab, second)],
        [pinned(ROWS * CHUNKS)],
        [pltpu.VMEM((ROWS * WIDE, LANES), F32), plan, terms_ref, sem],
    )
    (out,) = call(
        last_kernel,
        [(a, "v") for a in (mine, first, second, rest)],
        [jax.ShapeDtypeStruct((1024, LANES), F32)],
    )
    return out.reshape(8, CHUNKS, 8, LANES).transpose(0, 2, 1, 3).reshape(ROWS, CHUNKS * LANES)


def solution(mesh):
    placed = (P("freq", "tm"), P(None, "freq"), P(None, "freq"), P(None, "freq"))
    return jax.shard_map(
        on_device, mesh=mesh, in_specs=placed, out_specs=P("freq", "tm"), check_vma=False
    )
```

```python
import functools
import math

import jax
import jax.numpy as jnp
from jax import lax
from jax.experimental import pallas as pl
from jax.experimental.pallas import tpu as pltpu
from jax.sharding import PartitionSpec as P

LOCAL = 6
LEVELS = 9
ROWS = 64
LANES = 128
CHUNKS = 16
PITCH = 24
PACKED = 18
WIDE = 20
TO_PAIR, TO_CROSS = 12, 12
PAIR_REST, CROSS_REST = 19 - TO_PAIR, 19 - TO_CROSS
PART = 10
SCALE = 1.0 / math.sqrt(2.0**LEVELS)
F32 = jnp.float32


def lanes(count):
    return lax.broadcasted_iota(jnp.int32, (count, LANES), 1)


def place():
    at = lax.axis_index("freq")
    return [jnp.bitwise_and(lax.shift_right_logical(at, bit), 1) for bit in range(3)]


def turned(here, before, turn):
    return pltpu.roll(
        jnp.where(lanes(here.shape[0]) < LANES - turn, here, before), turn, axis=1
    )


def level_codes(low, high, lag):
    row = lax.broadcasted_iota(jnp.int32, (LEVELS, ROWS), 1)
    level = lax.broadcasted_iota(jnp.int32, (LEVELS, ROWS), 0)
    span = lax.shift_left(2, level)
    local = level < LOCAL
    start = jnp.where(local, jnp.bitwise_and(row, -span), 0)
    half = jnp.where(local, lax.shift_right_logical(span, 1), 0)
    pitch = jnp.where(local, PITCH, PACKED)
    return (start + low) * pitch + (start + half + high) * pitch * 2048 + lag * 2**22


def opened(code):
    return (
        jnp.bitwise_and(code, 2047),
        jnp.bitwise_and(lax.shift_right_logical(code, 11), 2047),
        lax.shift_right_logical(code, 22),
    )


def pieces(src, code, skip, high_skip, spans):
    low_at, high_at, turn = opened(code)
    return [
        src[pl.ds(low_at + (skip + first), count), :]
        + turned(
            src[pl.ds(high_at + (high_skip + first), count), :],
            src[pl.ds(high_at + (high_skip + first - 1), count), :],
            turn,
        )
        for first, count in spans
    ]


WHOLE = ((0, 8), (8, 8), (16, 1))


def main_kernel(
    x_h, low_h, high_h, lag_h, out, tab, codes, x, low, high, lag, plan, buf_a, buf_b, sems
):
    copies = [
        pltpu.make_async_copy(source, target, sems.at[at])
        for at, (source, target) in enumerate(((low_h, low), (high_h, high), (lag_h, lag)))
    ]
    parts = [
        pltpu.make_async_copy(
            x_h.at[pl.ds(part * 256, 256)], x.at[pl.ds(part * 256, 256)], sems.at[3 + part]
        )
        for part in range(4)
    ]
    for copy in copies + parts:
        copy.start()
    for row in range(ROWS):
        out[pl.ds(row * PACKED, 1), :] = jnp.zeros((1, LANES), F32)
    for row in range(ROWS + 1):
        for buf in (buf_a, buf_b):
            buf[pl.ds(row * PITCH, 8), :] = jnp.zeros((8, LANES), F32)
    for copy in copies:
        copy.wait()
    plan[...] = jnp.zeros_like(plan)
    plan[0:LEVELS, 0:ROWS] = level_codes(low[...], high[...], lag[...])
    planned = pltpu.make_async_copy(plan, codes, sems.at[7])
    planned.start()
    tab[...] = jnp.zeros_like(tab)
    for at, table in enumerate((low, high, lag)):
        tab[pl.ds(2 * at, 2), 0:ROWS] = table[LOCAL + 1 : LEVELS, :]
    none = jnp.zeros((1, LANES), F32)
    for part, copy in enumerate(parts):
        copy.wait()
        for row in range(part * 16, part * 16 + 16, 2):
            at = (row // 8) * 128 + row % 8
            low_row = x[pl.ds(at, CHUNKS, stride=8), :]
            high_row = x[pl.ds(at + 1, CHUNKS, stride=8), :]
            before = jnp.concatenate([none, high_row[: CHUNKS - 1]], axis=0)
            to = row * PITCH + 8
            buf_a[pl.ds(to, CHUNKS), :] = low_row + high_row
            buf_a[pl.ds(to + PITCH, CHUNKS), :] = low_row + turned(high_row, before, 1)
            buf_a[pl.ds(to + PITCH + CHUNKS, 1), :] = turned(none, high_row[CHUNKS - 1 :], 1)
    planned.wait()
    src, dst = buf_a, buf_b
    for level in range(1, LOCAL):
        last = level == LOCAL - 1
        for row in range(ROWS):
            to = row * PACKED + 1 if last else row * PITCH + 8
            for (first, count), piece in zip(WHOLE, pieces(src, codes[level, row], 8, 8, WHOLE)):
                (out if last else dst)[pl.ds(to + first, count), :] = piece
        src, dst = dst, src


def term_codes(tab7, tab8, odd, upper, pitch):
    def rows(tab, at):
        return jnp.broadcast_to(tab[at : at + 1, :], (8, LANES))

    via = jnp.where(upper == 1, rows(tab8, 3), rows(tab8, 1))
    late = jnp.where(upper == 1, rows(tab8, 5), 0)
    source = jnp.where(odd == 1, rows(tab7, 2), rows(tab7, 0))
    later = jnp.where(odd == 1, rows(tab7, 4), 0)
    late = late + jnp.take_along_axis(later, via, axis=1)
    source = jnp.take_along_axis(source, via, axis=1)
    at = source * pitch - lax.shift_right_logical(late, 7)
    return (at * LANES + jnp.bitwise_and(late, LANES - 1))[0:1]


def shares(src, ahead, codes, which, count, put):
    for row in range(ROWS):
        code = codes[which, row]
        at = lax.shift_right_arithmetic(code, 7)
        turn = jnp.bitwise_and(code, LANES - 1)
        for first in range(0, count, 8):
            size = min(8, count - first)
            to = ahead + first
            value = turned(
                src[pl.ds(at + to, size), :], src[pl.ds(at + (to - 1), size), :], turn
            )
            put(row * count + first, size, value)


def into(out):
    def put(at, size, value):
        out[pl.ds(at, size), :] = value

    return put


def core_main_kernel(own, partner, codes, tab, l6, to_pair, to_cross, edge, both):
    core = place()[0]
    size = own.shape[0]
    both[pl.ds(pl.multiple_of(core * size, 8), size), :] = own[...]
    both[pl.ds(pl.multiple_of((1 - core) * size, 8), size), :] = partner[...]
    for message in (to_pair, to_cross):
        message[0:8, :] = tab[...].astype(F32)
    for row in range(ROWS):
        first, second, past = pieces(both, codes[LOCAL, row], 1, size + 1, WHOLE)
        l6[pl.ds(row * CHUNKS, 8), :] = first
        l6[pl.ds(row * CHUNKS + 8, 8), :] = second
        edge[pl.ds(row * 4, 3), :] = second[5:8]
        edge[pl.ds(row * 4 + 3, 1), :] = past
        at = 8 + row * TO_PAIR
        to_pair[pl.ds(at, TO_PAIR - 8), :] = first[16 - TO_PAIR :]
        to_pair[pl.ds(at + TO_PAIR - 8, 8), :] = second
        at = 8 + row * TO_CROSS
        to_cross[pl.ds(at, 7), :] = first[1:8]
        to_cross[pl.ds(at + 7, TO_CROSS - 7), :] = second[0 : TO_CROSS - 7]


def history_kernel(l6, edge, whole, pair_rest, cross_rest):
    inner = lax.axis_index("tm") > 0
    for row in range(ROWS):
        at = row * WIDE
        ahead = jnp.where(inner, edge[pl.ds(row * 4, 4), :], 0.0)
        block = l6[pl.ds(row * CHUNKS, CHUNKS), :]
        whole[pl.ds(at, 1), :] = jnp.zeros((1, LANES), F32)
        whole[pl.ds(at + 1, 3), :] = ahead[0:3]
        whole[pl.ds(at + 4, 1), :] = ahead[3:4] + block[0:1]
        whole[pl.ds(at + 5, CHUNKS - 1), :] = block[1:]
        to = row * PAIR_REST
        pair_rest[pl.ds(to, 3), :] = ahead[0:3]
        pair_rest[pl.ds(to + 3, 1), :] = ahead[3:4] + block[0:1]
        pair_rest[pl.ds(to + 4, PAIR_REST - 4), :] = block[1 : PAIR_REST - 3]
        to = row * CROSS_REST
        cross_rest[pl.ds(to, 3), :] = ahead[0:3]
        cross_rest[pl.ds(to + 3, 1), :] = ahead[3:4] + block[0:1]
        cross_rest[pl.ds(to + 4, CROSS_REST - 4), :] = block[TO_CROSS + 1 :]


def tables_of(message):
    return message[0:8, :].astype(jnp.int32)


def relay_kernel(pair, cross, for_pair, for_cross, terms, plan, sem):
    _, odd, upper = place()
    pair_tab, cross_tab = tables_of(pair), tables_of(cross)
    plan[...] = jnp.zeros_like(plan)
    plan[0:1, :] = term_codes(cross_tab, pair_tab, 1 - odd, 1 - upper, TO_CROSS)
    plan[1:2, :] = term_codes(pair_tab, cross_tab, 1 - odd, upper, TO_PAIR)
    plan[2:3, :] = term_codes(cross_tab, pair_tab, 1 - odd, 1 - upper, 8)
    copy = pltpu.make_async_copy(plan, terms, sem)
    copy.start()
    for_pair[ROWS * (PART - 4) :, :] = cross[0:8, :]
    copy.wait()
    shares(cross, 8 + 3, terms, 0, PART - 4, into(for_pair))
    shares(pair, 8 + TO_PAIR - 16 + PART, terms, 1, 16 - PART, into(for_cross))


def first_relay_kernel(cross, cross_rest, terms, _, for_pair, buf):
    for row in range(ROWS):
        buf[pl.ds(row * 8 + 1, 4), :] = cross_rest[pl.ds(row * CROSS_REST, 4), :]
        buf[pl.ds(row * 8 + 5, 3), :] = cross[pl.ds(8 + row * TO_CROSS, 3), :]
    shares(buf, 4, terms, 2, 4, into(for_pair))


def direct_kernel(whole, pair, pair_rest, cross, cross_rest, tab, relay, out, pair_buf, buf, plan, terms, sem):
    _, odd, upper = place()
    own, other = tab[...], relay[ROWS * (PART - 4) :, :].astype(jnp.int32)
    plan[...] = jnp.zeros_like(plan)
    plan[0:1, :] = term_codes(own, own, odd, upper, WIDE)
    plan[1:2, :] = term_codes(own, own, 1 - odd, upper, WIDE)
    plan[2:3, :] = term_codes(other, own, 1 - odd, 1 - upper, WIDE)
    copy = pltpu.make_async_copy(plan, terms, sem)
    copy.start()
    for row in range(ROWS):
        to, rest = row * WIDE, row * CROSS_REST
        pair_buf[pl.ds(to + 1, PAIR_REST), :] = pair_rest[pl.ds(row * PAIR_REST, PAIR_REST), :]
        pair_buf[pl.ds(to + 1 + PAIR_REST, TO_PAIR), :] = pair[
            pl.ds(8 + row * TO_PAIR, TO_PAIR), :
        ]
        buf[pl.ds(to + 1, 4), :] = cross_rest[pl.ds(rest, 4), :]
        buf[pl.ds(to + 5, TO_CROSS), :] = cross[pl.ds(8 + row * TO_CROSS, TO_CROSS), :]
        buf[pl.ds(to + 5 + TO_CROSS, CROSS_REST - 4), :] = cross_rest[
            pl.ds(rest + 4, CROSS_REST - 4), :
        ]
    copy.wait()
    for row in range(ROWS):
        found = []
        for which in range(3):
            code = terms[which, row]
            found.append((lax.shift_right_arithmetic(code, 7), jnp.bitwise_and(code, LANES - 1)))
        for first in (0, 8):
            to = 4 + first
            total = None
            for src, (at, turn) in zip((whole, pair_buf, buf), found):
                term = turned(src[pl.ds(at + to, 8), :], src[pl.ds(at + (to - 1), 8), :], turn)
                total = term if total is None else total + term
            out[pl.ds(row * CHUNKS + first, 8), :] = total


def last_kernel(mine, first, second, rest, out, buf, sems):
    copies = []
    for part in range(4):
        for row in range(part * 16, part * 16 + 16):
            at = (row // 8) * 128 + row % 8
            spans = (first, 0, 4), (second, 4, PART - 4), (rest, PART, 16 - PART)
            for arrived, chunk, count in spans:
                value = (
                    mine[pl.ds(row * CHUNKS + chunk, count), :]
                    + arrived[pl.ds(row * count, count), :]
                )
                buf[pl.ds(at + 8 * chunk, count, stride=8), :] = value * SCALE
        here = pl.ds(part * 256, 256)
        copies.append(pltpu.make_async_copy(buf.at[here], out.at[here], sems.at[part]))
        copies[-1].start()
    for copy in copies:
        copy.wait()


def call(kernel, ins, outs, scratch=()):
    pins = {"v": pltpu.VMEM, "t": pltpu.SMEM, "h": pltpu.HBM}
    kinds = {"v": pltpu.VMEM, "t": pltpu.SMEM, "h": pltpu.HBM}
    values = [
        pltpu.with_memory_space_constraint(a, pins[where]) if where in pins else a for a, where in ins
    ]
    return pl.pallas_call(
        kernel,
        out_shape=outs,
        in_specs=[pl.BlockSpec(memory_space=kinds[where]) for _, where in ins],
        out_specs=[pl.BlockSpec(memory_space=getattr(o, "memory_space", pltpu.VMEM)) for o in outs],
        scratch_shapes=list(scratch),
        compiler_params=pltpu.CompilerParams(vmem_limit_bytes=16 * 2**20),
    )(*values)


def pinned(sublanes, lane_count=LANES, dtype=F32):
    return pltpu.VMEM((sublanes, lane_count), dtype)


def swap(bit):
    return [(i, i ^ bit) for i in range(64)]


def on_device(x, low, high, lag):
    tiles = x.reshape(8, 8, CHUNKS, LANES).transpose(0, 2, 1, 3).reshape(1024, LANES)
    sem = pltpu.SemaphoreType.DMA
    ints = jnp.int32
    by_pair, by_cross = swap(2), swap(6)
    plan, terms_ref = pltpu.VMEM((8, LANES), ints), pltpu.SMEM((8, LANES), ints)

    l5, own_tab, codes = call(
        main_kernel,
        [(a, "h") for a in (tiles, low, high, lag)],
        [pinned(ROWS * PACKED), pinned(8, LANES, ints), pltpu.SMEM((16, LANES), ints)],
        [pltpu.VMEM((1024, LANES), F32)]
        + [pltpu.VMEM((LEVELS, ROWS), ints)] * 3
        + [pltpu.VMEM((16, LANES), ints)]
        + [pltpu.VMEM((ROWS * PITCH + 8, LANES), F32)] * 2
        + [sem((8,))],
    )
    l5_far = lax.ppermute(l5, "freq", swap(1))
    l6, pair, cross, edge = call(
        core_main_kernel,
        [(l5, "v"), (l5_far, "v"), (codes, "t"), (own_tab, "v")],
        [pinned(1024), pinned(8 + ROWS * TO_PAIR), pinned(8 + ROWS * TO_CROSS), pinned(ROWS * 4)],
        [pltpu.VMEM((2 * ROWS * PACKED, LANES), F32)],
    )
    cross = lax.ppermute(cross, "freq", by_cross)
    pair = lax.ppermute(pair, "freq", by_pair)
    edge = lax.ppermute(edge, "tm", [(i, (i + 1) % 4) for i in range(4)])

    whole, pair_rest, cross_rest = call(
        history_kernel,
        [(l6, "v"), (edge, "v")],
        [pinned(ROWS * WIDE), pinned(ROWS * PAIR_REST), pinned(ROWS * CROSS_REST)],
    )
    cross_rest = lax.ppermute(cross_rest, "freq", by_cross)
    pair_rest = lax.ppermute(pair_rest, "freq", by_pair)

    for_pair, for_cross, terms = call(
        relay_kernel,
        [(pair, "v"), (cross, "v")],
        [pinned(ROWS * (PART - 4) + 8), pinned(ROWS * (16 - PART)), terms_ref],
        [plan, sem],
    )
    second = lax.ppermute(for_pair, "freq", by_pair)
    rest = lax.ppermute(for_cross, "freq", by_cross)

    (for_pair,) = call(
        first_relay_kernel,
        [(cross, "v"), (cross_rest, "v"), (terms, "t"), (pair_rest, "v")],
        [pinned(ROWS * 4)],
        [pltpu.VMEM((512, LANES), F32)],
    )
    first = lax.ppermute(for_pair, "freq", by_pair)

    (mine,) = call(
        direct_kernel,
        [(a, "v") for a in (whole, pair, pair_rest, cross, cross_rest, own_tab, second)],
        [pinned(ROWS * CHUNKS)],
        [pltpu.VMEM((ROWS * WIDE, LANES), F32)] * 2 + [plan, terms_ref, sem],
    )
    (out,) = call(
        last_kernel,
        [(a, "v") for a in (mine, first, second, rest)],
        [pltpu.HBM((1024, LANES), F32)],
        [pltpu.VMEM((1024, LANES), F32), sem((4,))],
    )
    return out.reshape(8, CHUNKS, 8, LANES).transpose(0, 2, 1, 3).reshape(ROWS, CHUNKS * LANES)


def solution(mesh):
    placed = (P("freq", "tm"), P(None, "freq"), P(None, "freq"), P(None, "freq"))
    return jax.shard_map(
        on_device, mesh=mesh, in_specs=placed, out_specs=P("freq", "tm"), check_vma=False
    )
```

```python
import functools
import math

import jax
import jax.numpy as jnp
from jax import lax
from jax.experimental import pallas as pl
from jax.experimental.pallas import tpu as pltpu
from jax.sharding import PartitionSpec as P

LOCAL = 6
LEVELS = 9
ROWS = 64
LANES = 128
CHUNKS = 16
PITCH = 24
PACKED = 18
WIDE = 20
PART = 8
TO_PAIR, TO_CROSS, TURN = 19 - PART, PART - 1, PART + 4
SCALE = 1.0 / math.sqrt(2.0**LEVELS)
F32 = jnp.float32


def lanes(count):
    return lax.broadcasted_iota(jnp.int32, (count, LANES), 1)


def place():
    at = lax.axis_index("freq")
    return [jnp.bitwise_and(lax.shift_right_logical(at, bit), 1) for bit in range(3)]


def turned(here, before, turn):
    return pltpu.roll(
        jnp.where(lanes(here.shape[0]) < LANES - turn, here, before), turn, axis=1
    )


def level_codes(low, high, lag):
    row = lax.broadcasted_iota(jnp.int32, (LEVELS, ROWS), 1)
    level = lax.broadcasted_iota(jnp.int32, (LEVELS, ROWS), 0)
    span = lax.shift_left(2, level)
    local = level < LOCAL
    start = jnp.where(local, jnp.bitwise_and(row, -span), 0)
    half = jnp.where(local, lax.shift_right_logical(span, 1), 0)
    pitch = jnp.where(local, PITCH, PACKED)
    return (start + low) * pitch + (start + half + high) * pitch * 2048 + lag * 2**22


def opened(code):
    return (
        jnp.bitwise_and(code, 2047),
        jnp.bitwise_and(lax.shift_right_logical(code, 11), 2047),
        lax.shift_right_logical(code, 22),
    )


def pieces(src, code, skip, high_skip, spans):
    low_at, high_at, turn = opened(code)
    return [
        src[pl.ds(low_at + (skip + first), count), :]
        + turned(
            src[pl.ds(high_at + (high_skip + first), count), :],
            src[pl.ds(high_at + (high_skip + first - 1), count), :],
            turn,
        )
        for first, count in spans
    ]


WHOLE = ((0, 8), (8, 8), (16, 1))


def main_kernel(
    x_h, low_h, high_h, lag_h, out, tab, codes, x, low, high, lag, plan, buf_a, buf_b, sems
):
    copies = [
        pltpu.make_async_copy(source, target, sems.at[at])
        for at, (source, target) in enumerate(((low_h, low), (high_h, high), (lag_h, lag)))
    ]
    parts = [
        pltpu.make_async_copy(
            x_h.at[pl.ds(part * 256, 256)], x.at[pl.ds(part * 256, 256)], sems.at[3 + part]
        )
        for part in range(4)
    ]
    for copy in copies + parts:
        copy.start()
    for row in range(ROWS):
        out[pl.ds(row * PACKED, 1), :] = jnp.zeros((1, LANES), F32)
    for row in range(ROWS + 1):
        for buf in (buf_a, buf_b):
            buf[pl.ds(row * PITCH, 8), :] = jnp.zeros((8, LANES), F32)
    for copy in copies:
        copy.wait()
    plan[...] = jnp.zeros_like(plan)
    plan[0:LEVELS, 0:ROWS] = level_codes(low[...], high[...], lag[...])
    planned = pltpu.make_async_copy(plan, codes, sems.at[7])
    planned.start()
    tab[...] = jnp.zeros_like(tab)
    for at, table in enumerate((low, high, lag)):
        tab[pl.ds(2 * at, 2), 0:ROWS] = table[LOCAL + 1 : LEVELS, :]
    none = jnp.zeros((1, LANES), F32)
    for part, copy in enumerate(parts):
        copy.wait()
        for row in range(part * 16, part * 16 + 16, 2):
            at = (row // 8) * 128 + row % 8
            low_row = x[pl.ds(at, CHUNKS, stride=8), :]
            high_row = x[pl.ds(at + 1, CHUNKS, stride=8), :]
            before = jnp.concatenate([none, high_row[: CHUNKS - 1]], axis=0)
            to = row * PITCH + 8
            buf_a[pl.ds(to, CHUNKS), :] = low_row + high_row
            buf_a[pl.ds(to + PITCH, CHUNKS), :] = low_row + turned(high_row, before, 1)
            buf_a[pl.ds(to + PITCH + CHUNKS, 1), :] = turned(none, high_row[CHUNKS - 1 :], 1)
    planned.wait()
    src, dst = buf_a, buf_b
    for level in range(1, LOCAL):
        last = level == LOCAL - 1
        for row in range(ROWS):
            to = row * PACKED + 1 if last else row * PITCH + 8
            for (first, count), piece in zip(WHOLE, pieces(src, codes[level, row], 8, 8, WHOLE)):
                (out if last else dst)[pl.ds(to + first, count), :] = piece
        src, dst = dst, src


def term_codes(tab7, tab8, odd, upper, pitch):
    def rows(tab, at):
        return jnp.broadcast_to(tab[at : at + 1, :], (8, LANES))

    via = jnp.where(upper == 1, rows(tab8, 3), rows(tab8, 1))
    late = jnp.where(upper == 1, rows(tab8, 5), 0)
    source = jnp.where(odd == 1, rows(tab7, 2), rows(tab7, 0))
    later = jnp.where(odd == 1, rows(tab7, 4), 0)
    late = late + jnp.take_along_axis(later, via, axis=1)
    source = jnp.take_along_axis(source, via, axis=1)
    at = source * pitch - lax.shift_right_logical(late, 7)
    return (at * LANES + jnp.bitwise_and(late, LANES - 1))[0:1]


def shares(src, ahead, codes, which, count, put):
    for row in range(ROWS):
        code = codes[which, row]
        at = lax.shift_right_arithmetic(code, 7)
        turn = jnp.bitwise_and(code, LANES - 1)
        for first in range(0, count, 8):
            size = min(8, count - first)
            to = ahead + first
            value = turned(
                src[pl.ds(at + to, size), :], src[pl.ds(at + (to - 1), size), :], turn
            )
            put(row * count + first, size, value)


def into(out):
    def put(at, size, value):
        out[pl.ds(at, size), :] = value

    return put


def core_main_kernel(own, partner, codes, tab, l6, to_pair, to_cross, edge, both):
    core = place()[0]
    size = own.shape[0]
    both[pl.ds(pl.multiple_of(core * size, 8), size), :] = own[...]
    both[pl.ds(pl.multiple_of((1 - core) * size, 8), size), :] = partner[...]
    for message in (to_pair, to_cross):
        message[0:8, :] = tab[...].astype(F32)
    for row in range(ROWS):
        first, second, past = pieces(both, codes[LOCAL, row], 1, size + 1, WHOLE)
        l6[pl.ds(row * CHUNKS, 8), :] = first
        l6[pl.ds(row * CHUNKS + 8, 8), :] = second
        edge[pl.ds(row * 4, 3), :] = second[5:8]
        edge[pl.ds(row * 4 + 3, 1), :] = past
        at = 8 + row * TO_PAIR
        to_pair[pl.ds(at, TO_PAIR - 8), :] = first[PART - 3 :]
        to_pair[pl.ds(at + TO_PAIR - 8, 8), :] = second
        at = 8 + row * TO_CROSS
        to_cross[pl.ds(at, TO_CROSS), :] = first[1:PART]


def history_kernel(l6, edge, whole, cross_rest):
    inner = lax.axis_index("tm") > 0
    for row in range(ROWS):
        at = row * WIDE
        ahead = jnp.where(inner, edge[pl.ds(row * 4, 4), :], 0.0)
        block = l6[pl.ds(row * CHUNKS, CHUNKS), :]
        whole[pl.ds(at, 1), :] = jnp.zeros((1, LANES), F32)
        for target, to in ((whole, at + 1), (cross_rest, row * 4)):
            target[pl.ds(to, 3), :] = ahead[0:3]
            target[pl.ds(to + 3, 1), :] = ahead[3:4] + block[0:1]
        whole[pl.ds(at + 5, CHUNKS - 1), :] = block[1:]


def tables_of(message):
    return message[0:8, :].astype(jnp.int32)


def onto(out):
    def put(at, size, value):
        out[pl.ds(at, size), :] += value

    return put


def relay_kernel(l6, pair, cross, for_pair, for_cross, terms, plan, sem):
    _, odd, upper = place()
    pair_tab, cross_tab = tables_of(pair), tables_of(cross)
    plan[...] = jnp.zeros_like(plan)
    plan[0:1, :] = term_codes(cross_tab, pair_tab, 1 - odd, 1 - upper, TO_CROSS)
    plan[1:2, :] = term_codes(pair_tab, cross_tab, 1 - odd, upper, TO_PAIR)
    plan[2:3, :] = term_codes(cross_tab, pair_tab, 1 - odd, 1 - upper, 8)
    plan[3:4, :] = term_codes(pair_tab, pair_tab, odd, upper, CHUNKS)
    plan[4:5, :] = term_codes(pair_tab, cross_tab, odd, upper, CHUNKS)
    plan[5:6, :] = term_codes(pair_tab, pair_tab, odd, upper, WIDE)
    copy = pltpu.make_async_copy(plan, terms, sem)
    copy.start()
    for_pair[ROWS * (PART - 4) :, :] = cross[0:8, :]
    copy.wait()
    shares(cross, 8 + 3, terms, 0, PART - 4, into(for_pair))
    shares(l6, 4, terms, 3, PART - 4, onto(for_pair))
    shares(pair, 8 + 3, terms, 1, 16 - PART, into(for_cross))
    shares(l6, PART, terms, 4, 16 - PART, onto(for_cross))


def first_relay_kernel(whole, cross, cross_rest, terms, for_pair, buf):
    for row in range(ROWS):
        buf[pl.ds(row * 8 + 1, 4), :] = cross_rest[pl.ds(row * 4, 4), :]
        buf[pl.ds(row * 8 + 5, 3), :] = cross[pl.ds(8 + row * TO_CROSS, 3), :]
    shares(buf, 4, terms, 2, 4, into(for_pair))
    shares(whole, 4, terms, 5, 4, onto(for_pair))


def direct_kernel(whole, pair, cross, cross_rest, tab, relay, out, buf, plan, terms, sem):
    _, odd, upper = place()
    own, other = tab[...], relay[ROWS * (PART - 4) :, :].astype(jnp.int32)
    plan[...] = jnp.zeros_like(plan)
    plan[0:1, :] = term_codes(own, own, odd, upper, WIDE)
    plan[1:2, :] = term_codes(own, own, 1 - odd, upper, TO_PAIR)
    plan[2:3, :] = term_codes(other, own, 1 - odd, 1 - upper, TURN)
    copy = pltpu.make_async_copy(plan, terms, sem)
    copy.start()
    for row in range(ROWS):
        to = row * TURN
        buf[pl.ds(to + 1, 4), :] = cross_rest[pl.ds(row * 4, 4), :]
        buf[pl.ds(to + 5, TO_CROSS), :] = cross[pl.ds(8 + row * TO_CROSS, TO_CROSS), :]
    copy.wait()
    for row in range(ROWS):
        found = []
        for which in range(3):
            code = terms[which, row]
            found.append((lax.shift_right_arithmetic(code, 7), jnp.bitwise_and(code, LANES - 1)))
        (own_at, own_turn), near, away = found
        for first, count, src, ahead, (at, turn) in (
            (0, PART, buf, 4, away),
            (PART, 16 - PART, pair, 8 + 3, near),
        ):
            to = 4 + first
            out[pl.ds(row * CHUNKS + first, count), :] = turned(
                whole[pl.ds(own_at + to, count), :],
                whole[pl.ds(own_at + (to - 1), count), :],
                own_turn,
            ) + turned(
                src[pl.ds(at + ahead, count), :], src[pl.ds(at + (ahead - 1), count), :], turn
            )


def last_kernel(mine, first, second, rest, out, buf, sems):
    copies = []
    for part in range(4):
        for row in range(part * 16, part * 16 + 16):
            at = (row // 8) * 128 + row % 8
            spans = (first, 0, 4), (second, 4, PART - 4), (rest, PART, 16 - PART)
            for arrived, chunk, count in spans:
                value = (
                    mine[pl.ds(row * CHUNKS + chunk, count), :]
                    + arrived[pl.ds(row * count, count), :]
                )
                buf[pl.ds(at + 8 * chunk, count, stride=8), :] = value * SCALE
        here = pl.ds(part * 256, 256)
        copies.append(pltpu.make_async_copy(buf.at[here], out.at[here], sems.at[part]))
        copies[-1].start()
    for copy in copies:
        copy.wait()


def call(kernel, ins, outs, scratch=()):
    pins = {"v": pltpu.VMEM, "t": pltpu.SMEM, "h": pltpu.HBM}
    kinds = {"v": pltpu.VMEM, "t": pltpu.SMEM, "h": pltpu.HBM}
    values = [
        pltpu.with_memory_space_constraint(a, pins[where]) if where in pins else a for a, where in ins
    ]
    return pl.pallas_call(
        kernel,
        out_shape=outs,
        in_specs=[pl.BlockSpec(memory_space=kinds[where]) for _, where in ins],
        out_specs=[pl.BlockSpec(memory_space=getattr(o, "memory_space", pltpu.VMEM)) for o in outs],
        scratch_shapes=list(scratch),
        compiler_params=pltpu.CompilerParams(vmem_limit_bytes=16 * 2**20),
    )(*values)


def pinned(sublanes, lane_count=LANES, dtype=F32):
    return pltpu.VMEM((sublanes, lane_count), dtype)


def swap(bit):
    return [(i, i ^ bit) for i in range(64)]


def on_device(x, low, high, lag):
    tiles = x.reshape(8, 8, CHUNKS, LANES).transpose(0, 2, 1, 3).reshape(1024, LANES)
    sem = pltpu.SemaphoreType.DMA
    ints = jnp.int32
    by_pair, by_cross = swap(2), swap(6)
    plan, terms_ref = pltpu.VMEM((8, LANES), ints), pltpu.SMEM((8, LANES), ints)

    l5, own_tab, codes = call(
        main_kernel,
        [(a, "h") for a in (tiles, low, high, lag)],
        [pinned(ROWS * PACKED), pinned(8, LANES, ints), pltpu.SMEM((16, LANES), ints)],
        [pltpu.VMEM((1024, LANES), F32)]
        + [pltpu.VMEM((LEVELS, ROWS), ints)] * 3
        + [pltpu.VMEM((16, LANES), ints)]
        + [pltpu.VMEM((ROWS * PITCH + 8, LANES), F32)] * 2
        + [sem((8,))],
    )
    l5_far = lax.ppermute(l5, "freq", swap(1))
    l6, pair, cross, edge = call(
        core_main_kernel,
        [(l5, "v"), (l5_far, "v"), (codes, "t"), (own_tab, "v")],
        [pinned(1024), pinned(8 + ROWS * TO_PAIR), pinned(8 + ROWS * TO_CROSS), pinned(ROWS * 4)],
        [pltpu.VMEM((2 * ROWS * PACKED, LANES), F32)],
    )
    cross = lax.ppermute(cross, "freq", by_cross)
    pair = lax.ppermute(pair, "freq", by_pair)
    edge = lax.ppermute(edge, "tm", [(i, (i + 1) % 4) for i in range(4)])

    whole, cross_rest = call(
        history_kernel,
        [(l6, "v"), (edge, "v")],
        [pinned(ROWS * WIDE), pinned(ROWS * 4)],
    )
    cross_rest = lax.ppermute(cross_rest, "freq", by_cross)

    for_pair, for_cross, terms = call(
        relay_kernel,
        [(l6, "v"), (pair, "v"), (cross, "v")],
        [pinned(ROWS * (PART - 4) + 8), pinned(ROWS * (16 - PART)), terms_ref],
        [plan, sem],
    )
    second = lax.ppermute(for_pair, "freq", by_pair)
    rest = lax.ppermute(for_cross, "freq", by_cross)

    (for_pair,) = call(
        first_relay_kernel,
        [(whole, "v"), (cross, "v"), (cross_rest, "v"), (terms, "t")],
        [pinned(ROWS * 4)],
        [pltpu.VMEM((512, LANES), F32)],
    )
    first = lax.ppermute(for_pair, "freq", by_pair)

    (mine,) = call(
        direct_kernel,
        [(a, "v") for a in (whole, pair, cross, cross_rest, own_tab, second)],
        [pinned(ROWS * CHUNKS)],
        [pltpu.VMEM((ROWS * TURN, LANES), F32), plan, terms_ref, sem],
    )
    (out,) = call(
        last_kernel,
        [(a, "v") for a in (mine, first, second, rest)],
        [pltpu.HBM((1024, LANES), F32)],
        [pltpu.VMEM((1024, LANES), F32), sem((4,))],
    )
    return out.reshape(8, CHUNKS, 8, LANES).transpose(0, 2, 1, 3).reshape(ROWS, CHUNKS * LANES)


def solution(mesh):
    placed = (P("freq", "tm"), P(None, "freq"), P(None, "freq"), P(None, "freq"))
    return jax.shard_map(
        on_device, mesh=mesh, in_specs=placed, out_specs=P("freq", "tm"), check_vma=False
    )
```

```python
import functools
import math

import jax
import jax.numpy as jnp
from jax import lax
from jax.experimental import pallas as pl
from jax.experimental.pallas import tpu as pltpu
from jax.sharding import PartitionSpec as P

LOCAL = 6
LEVELS = 9
ROWS = 64
LANES = 128
CHUNKS = 16
PITCH = 24
PACKED = 18
WIDE = 20
PART = 10
TO_PAIR, TO_CROSS, TURN = 19 - PART, PART - 1, PART + 4
SCALE = 1.0 / math.sqrt(2.0**LEVELS)
F32 = jnp.float32


def lanes(count):
    return lax.broadcasted_iota(jnp.int32, (count, LANES), 1)


def place():
    at = lax.axis_index("freq")
    return [jnp.bitwise_and(lax.shift_right_logical(at, bit), 1) for bit in range(3)]


def turned(here, before, turn):
    return pltpu.roll(
        jnp.where(lanes(here.shape[0]) < LANES - turn, here, before), turn, axis=1
    )


def level_codes(low, high, lag):
    row = lax.broadcasted_iota(jnp.int32, (LEVELS, ROWS), 1)
    level = lax.broadcasted_iota(jnp.int32, (LEVELS, ROWS), 0)
    span = lax.shift_left(2, level)
    local = level < LOCAL
    start = jnp.where(local, jnp.bitwise_and(row, -span), 0)
    half = jnp.where(local, lax.shift_right_logical(span, 1), 0)
    pitch = jnp.where(local, PITCH, PACKED)
    return (start + low) * pitch + (start + half + high) * pitch * 2048 + lag * 2**22


def opened(code):
    return (
        jnp.bitwise_and(code, 2047),
        jnp.bitwise_and(lax.shift_right_logical(code, 11), 2047),
        lax.shift_right_logical(code, 22),
    )


def pieces(src, code, skip, high_skip, spans):
    low_at, high_at, turn = opened(code)
    return [
        src[pl.ds(low_at + (skip + first), count), :]
        + turned(
            src[pl.ds(high_at + (high_skip + first), count), :],
            src[pl.ds(high_at + (high_skip + first - 1), count), :],
            turn,
        )
        for first, count in spans
    ]


WHOLE = ((0, 8), (8, 8), (16, 1))


def main_kernel(
    x_h, low_h, high_h, lag_h, out, tab, codes, x, low, high, lag, plan, buf_a, buf_b, sems
):
    copies = [
        pltpu.make_async_copy(source, target, sems.at[at])
        for at, (source, target) in enumerate(((low_h, low), (high_h, high), (lag_h, lag)))
    ]
    parts = [
        pltpu.make_async_copy(
            x_h.at[pl.ds(part * 256, 256)], x.at[pl.ds(part * 256, 256)], sems.at[3 + part]
        )
        for part in range(4)
    ]
    for copy in copies + parts:
        copy.start()
    for row in range(ROWS):
        out[pl.ds(row * PACKED, 1), :] = jnp.zeros((1, LANES), F32)
    for row in range(ROWS + 1):
        for buf in (buf_a, buf_b):
            buf[pl.ds(row * PITCH, 8), :] = jnp.zeros((8, LANES), F32)
    for copy in copies:
        copy.wait()
    plan[...] = jnp.zeros_like(plan)
    plan[0:LEVELS, 0:ROWS] = level_codes(low[...], high[...], lag[...])
    planned = pltpu.make_async_copy(plan, codes, sems.at[7])
    planned.start()
    tab[...] = jnp.zeros_like(tab)
    for at, table in enumerate((low, high, lag)):
        tab[pl.ds(2 * at, 2), 0:ROWS] = table[LOCAL + 1 : LEVELS, :]
    none = jnp.zeros((1, LANES), F32)
    for part, copy in enumerate(parts):
        copy.wait()
        for row in range(part * 16, part * 16 + 16, 2):
            at = (row // 8) * 128 + row % 8
            low_row = x[pl.ds(at, CHUNKS, stride=8), :]
            high_row = x[pl.ds(at + 1, CHUNKS, stride=8), :]
            before = jnp.concatenate([none, high_row[: CHUNKS - 1]], axis=0)
            to = row * PITCH + 8
            buf_a[pl.ds(to, CHUNKS), :] = low_row + high_row
            buf_a[pl.ds(to + PITCH, CHUNKS), :] = low_row + turned(high_row, before, 1)
            buf_a[pl.ds(to + PITCH + CHUNKS, 1), :] = turned(none, high_row[CHUNKS - 1 :], 1)
    planned.wait()
    src, dst = buf_a, buf_b
    for level in range(1, LOCAL):
        last = level == LOCAL - 1
        for row in range(ROWS):
            to = row * PACKED + 1 if last else row * PITCH + 8
            for (first, count), piece in zip(WHOLE, pieces(src, codes[level, row], 8, 8, WHOLE)):
                (out if last else dst)[pl.ds(to + first, count), :] = piece
        src, dst = dst, src


def term_codes(tab7, tab8, odd, upper, pitch):
    def rows(tab, at):
        return jnp.broadcast_to(tab[at : at + 1, :], (8, LANES))

    via = jnp.where(upper == 1, rows(tab8, 3), rows(tab8, 1))
    late = jnp.where(upper == 1, rows(tab8, 5), 0)
    source = jnp.where(odd == 1, rows(tab7, 2), rows(tab7, 0))
    later = jnp.where(odd == 1, rows(tab7, 4), 0)
    late = late + jnp.take_along_axis(later, via, axis=1)
    source = jnp.take_along_axis(source, via, axis=1)
    at = source * pitch - lax.shift_right_logical(late, 7)
    return (at * LANES + jnp.bitwise_and(late, LANES - 1))[0:1]


def shares(src, ahead, codes, which, count, put):
    for row in range(ROWS):
        code = codes[which, row]
        at = lax.shift_right_arithmetic(code, 7)
        turn = jnp.bitwise_and(code, LANES - 1)
        for first in range(0, count, 8):
            size = min(8, count - first)
            to = ahead + first
            value = turned(
                src[pl.ds(at + to, size), :], src[pl.ds(at + (to - 1), size), :], turn
            )
            put(row * count + first, size, value)


def into(out):
    def put(at, size, value):
        out[pl.ds(at, size), :] = value

    return put


def core_main_kernel(own, partner, codes, tab, l6, to_pair, to_cross, edge, both):
    core = place()[0]
    size = own.shape[0]
    both[pl.ds(pl.multiple_of(core * size, 8), size), :] = own[...]
    both[pl.ds(pl.multiple_of((1 - core) * size, 8), size), :] = partner[...]
    for message in (to_pair, to_cross):
        message[0:8, :] = tab[...].astype(F32)
    for row in range(ROWS):
        first, second, past = pieces(both, codes[LOCAL, row], 1, size + 1, WHOLE)
        l6[pl.ds(row * CHUNKS, 8), :] = first
        l6[pl.ds(row * CHUNKS + 8, 8), :] = second
        edge[pl.ds(row * 4, 3), :] = second[5:8]
        edge[pl.ds(row * 4 + 3, 1), :] = past
        at = 8 + row * TO_PAIR
        to_pair[pl.ds(at, TO_PAIR - 8), :] = first[PART - 3 :]
        to_pair[pl.ds(at + TO_PAIR - 8, 8), :] = second
        at = 8 + row * TO_CROSS
        to_cross[pl.ds(at, 7), :] = first[1:8]
        to_cross[pl.ds(at + 7, PART - 8), :] = second[0 : PART - 8]


def history_kernel(l6, edge, whole, cross_rest):
    inner = lax.axis_index("tm") > 0
    for row in range(ROWS):
        at = row * WIDE
        ahead = jnp.where(inner, edge[pl.ds(row * 4, 4), :], 0.0)
        block = l6[pl.ds(row * CHUNKS, CHUNKS), :]
        whole[pl.ds(at, 1), :] = jnp.zeros((1, LANES), F32)
        for target, to in ((whole, at + 1), (cross_rest, row * 4)):
            target[pl.ds(to, 3), :] = ahead[0:3]
            target[pl.ds(to + 3, 1), :] = ahead[3:4] + block[0:1]
        whole[pl.ds(at + 5, CHUNKS - 1), :] = block[1:]


def tables_of(message):
    return message[0:8, :].astype(jnp.int32)


def onto(out):
    def put(at, size, value):
        out[pl.ds(at, size), :] += value

    return put


def relay_kernel(l6, pair, cross, for_pair, for_cross, terms, plan, sem):
    _, odd, upper = place()
    pair_tab, cross_tab = tables_of(pair), tables_of(cross)
    plan[...] = jnp.zeros_like(plan)
    plan[0:1, :] = term_codes(cross_tab, pair_tab, 1 - odd, 1 - upper, TO_CROSS)
    plan[1:2, :] = term_codes(pair_tab, cross_tab, 1 - odd, upper, TO_PAIR)
    plan[2:3, :] = term_codes(cross_tab, pair_tab, 1 - odd, 1 - upper, 8)
    plan[3:4, :] = term_codes(pair_tab, pair_tab, odd, upper, CHUNKS)
    plan[4:5, :] = term_codes(pair_tab, cross_tab, odd, upper, CHUNKS)
    plan[5:6, :] = term_codes(pair_tab, pair_tab, odd, upper, WIDE)
    copy = pltpu.make_async_copy(plan, terms, sem)
    copy.start()
    for_pair[ROWS * (PART - 4) :, :] = cross[0:8, :]
    copy.wait()
    shares(cross, 8 + 3, terms, 0, PART - 4, into(for_pair))
    shares(l6, 4, terms, 3, PART - 4, onto(for_pair))
    shares(pair, 8 + 3, terms, 1, 16 - PART, into(for_cross))
    shares(l6, PART, terms, 4, 16 - PART, onto(for_cross))


def first_relay_kernel(whole, cross, cross_rest, terms, for_pair, buf):
    for row in range(ROWS):
        buf[pl.ds(row * 8 + 1, 4), :] = cross_rest[pl.ds(row * 4, 4), :]
        buf[pl.ds(row * 8 + 5, 3), :] = cross[pl.ds(8 + row * TO_CROSS, 3), :]
    shares(buf, 4, terms, 2, 4, into(for_pair))
    shares(whole, 4, terms, 5, 4, onto(for_pair))


def direct_kernel(whole, pair, cross, cross_rest, tab, relay, out, buf, plan, terms, sem):
    _, odd, upper = place()
    own, other = tab[...], relay[ROWS * (PART - 4) :, :].astype(jnp.int32)
    plan[...] = jnp.zeros_like(plan)
    plan[0:1, :] = term_codes(own, own, odd, upper, WIDE)
    plan[1:2, :] = term_codes(own, own, 1 - odd, upper, TO_PAIR)
    plan[2:3, :] = term_codes(other, own, 1 - odd, 1 - upper, TURN)
    copy = pltpu.make_async_copy(plan, terms, sem)
    copy.start()
    for row in range(ROWS):
        to = row * TURN
        buf[pl.ds(to + 1, 4), :] = cross_rest[pl.ds(row * 4, 4), :]
        buf[pl.ds(to + 5, TO_CROSS), :] = cross[pl.ds(8 + row * TO_CROSS, TO_CROSS), :]
    copy.wait()
    for row in range(ROWS):
        found = []
        for which in range(3):
            code = terms[which, row]
            found.append((lax.shift_right_arithmetic(code, 7), jnp.bitwise_and(code, LANES - 1)))
        (own_at, own_turn), near, away = found
        for first, count, src, ahead, (at, turn) in (
            (0, PART, buf, 4, away),
            (PART, 16 - PART, pair, 8 + 3, near),
        ):
            to = 4 + first
            out[pl.ds(row * CHUNKS + first, count), :] = turned(
                whole[pl.ds(own_at + to, count), :],
                whole[pl.ds(own_at + (to - 1), count), :],
                own_turn,
            ) + turned(
                src[pl.ds(at + ahead, count), :], src[pl.ds(at + (ahead - 1), count), :], turn
            )


def last_kernel(mine, first, second, rest, out, buf, sems):
    copies = []
    for part in range(4):
        for row in range(part * 16, part * 16 + 16):
            at = (row // 8) * 128 + row % 8
            spans = (first, 0, 4), (second, 4, PART - 4), (rest, PART, 16 - PART)
            for arrived, chunk, count in spans:
                value = (
                    mine[pl.ds(row * CHUNKS + chunk, count), :]
                    + arrived[pl.ds(row * count, count), :]
                )
                buf[pl.ds(at + 8 * chunk, count, stride=8), :] = value * SCALE
        here = pl.ds(part * 256, 256)
        copies.append(pltpu.make_async_copy(buf.at[here], out.at[here], sems.at[part]))
        copies[-1].start()
    for copy in copies:
        copy.wait()


def call(kernel, ins, outs, scratch=()):
    pins = {"v": pltpu.VMEM, "t": pltpu.SMEM, "h": pltpu.HBM}
    kinds = {"v": pltpu.VMEM, "t": pltpu.SMEM, "h": pltpu.HBM}
    values = [
        pltpu.with_memory_space_constraint(a, pins[where]) if where in pins else a for a, where in ins
    ]
    return pl.pallas_call(
        kernel,
        out_shape=outs,
        in_specs=[pl.BlockSpec(memory_space=kinds[where]) for _, where in ins],
        out_specs=[pl.BlockSpec(memory_space=getattr(o, "memory_space", pltpu.VMEM)) for o in outs],
        scratch_shapes=list(scratch),
        compiler_params=pltpu.CompilerParams(vmem_limit_bytes=16 * 2**20),
    )(*values)


def pinned(sublanes, lane_count=LANES, dtype=F32):
    return pltpu.VMEM((sublanes, lane_count), dtype)


def swap(bit):
    return [(i, i ^ bit) for i in range(64)]


def on_device(x, low, high, lag):
    tiles = x.reshape(8, 8, CHUNKS, LANES).transpose(0, 2, 1, 3).reshape(1024, LANES)
    sem = pltpu.SemaphoreType.DMA
    ints = jnp.int32
    by_pair, by_cross = swap(2), swap(6)
    plan, terms_ref = pltpu.VMEM((8, LANES), ints), pltpu.SMEM((8, LANES), ints)

    l5, own_tab, codes = call(
        main_kernel,
        [(a, "h") for a in (tiles, low, high, lag)],
        [pinned(ROWS * PACKED), pinned(8, LANES, ints), pltpu.SMEM((16, LANES), ints)],
        [pltpu.VMEM((1024, LANES), F32)]
        + [pltpu.VMEM((LEVELS, ROWS), ints)] * 3
        + [pltpu.VMEM((16, LANES), ints)]
        + [pltpu.VMEM((ROWS * PITCH + 8, LANES), F32)] * 2
        + [sem((8,))],
    )
    l5_far = lax.ppermute(l5, "freq", swap(1))
    l6, pair, cross, edge = call(
        core_main_kernel,
        [(l5, "v"), (l5_far, "v"), (codes, "t"), (own_tab, "v")],
        [pinned(1024), pinned(8 + ROWS * TO_PAIR), pinned(8 + ROWS * TO_CROSS), pinned(ROWS * 4)],
        [pltpu.VMEM((2 * ROWS * PACKED, LANES), F32)],
    )
    cross = lax.ppermute(cross, "freq", by_cross)
    pair = lax.ppermute(pair, "freq", by_pair)
    edge = lax.ppermute(edge, "tm", [(i, (i + 1) % 4) for i in range(4)])

    whole, cross_rest = call(
        history_kernel,
        [(l6, "v"), (edge, "v")],
        [pinned(ROWS * WIDE), pinned(ROWS * 4)],
    )
    cross_rest = lax.ppermute(cross_rest, "freq", by_cross)

    for_pair, for_cross, terms = call(
        relay_kernel,
        [(l6, "v"), (pair, "v"), (cross, "v")],
        [pinned(ROWS * (PART - 4) + 8), pinned(ROWS * (16 - PART)), terms_ref],
        [plan, sem],
    )
    second = lax.ppermute(for_pair, "freq", by_pair)
    rest = lax.ppermute(for_cross, "freq", by_cross)

    (for_pair,) = call(
        first_relay_kernel,
        [(whole, "v"), (cross, "v"), (cross_rest, "v"), (terms, "t")],
        [pinned(ROWS * 4)],
        [pltpu.VMEM((512, LANES), F32)],
    )
    first = lax.ppermute(for_pair, "freq", by_pair)

    (mine,) = call(
        direct_kernel,
        [(a, "v") for a in (whole, pair, cross, cross_rest, own_tab, second)],
        [pinned(ROWS * CHUNKS)],
        [pltpu.VMEM((ROWS * TURN, LANES), F32), plan, terms_ref, sem],
    )
    (out,) = call(
        last_kernel,
        [(a, "v") for a in (mine, first, second, rest)],
        [pltpu.HBM((1024, LANES), F32)],
        [pltpu.VMEM((1024, LANES), F32), sem((4,))],
    )
    return out.reshape(8, CHUNKS, 8, LANES).transpose(0, 2, 1, 3).reshape(ROWS, CHUNKS * LANES)


def solution(mesh):
    placed = (P("freq", "tm"), P(None, "freq"), P(None, "freq"), P(None, "freq"))
    return jax.shard_map(
        on_device, mesh=mesh, in_specs=placed, out_specs=P("freq", "tm"), check_vma=False
    )
```

```python
import functools
import math

import jax
import jax.numpy as jnp
from jax import lax
from jax.experimental import pallas as pl
from jax.experimental.pallas import tpu as pltpu
from jax.sharding import PartitionSpec as P

LOCAL = 6
LEVELS = 9
ROWS = 64
LANES = 128
CHUNKS = 16
PITCH = 24
PACKED = 18
WIDE = 20
PART = 10
TO_PAIR, TO_CROSS, TURN = 19 - PART, PART - 1, PART + 4
SCALE = 1.0 / math.sqrt(2.0**LEVELS)
F32 = jnp.float32


def lanes(count):
    return lax.broadcasted_iota(jnp.int32, (count, LANES), 1)


def place():
    at = lax.axis_index("freq")
    return [jnp.bitwise_and(lax.shift_right_logical(at, bit), 1) for bit in range(3)]


def turned(here, before, turn):
    return pltpu.roll(
        jnp.where(lanes(here.shape[0]) < LANES - turn, here, before), turn, axis=1
    )


def level_codes(low, high, lag):
    row = lax.broadcasted_iota(jnp.int32, (LEVELS, ROWS), 1)
    level = lax.broadcasted_iota(jnp.int32, (LEVELS, ROWS), 0)
    span = lax.shift_left(2, level)
    local = level < LOCAL
    start = jnp.where(local, jnp.bitwise_and(row, -span), 0)
    half = jnp.where(local, lax.shift_right_logical(span, 1), 0)
    pitch = jnp.where(local, PITCH, PACKED)
    return (start + low) * pitch + (start + half + high) * pitch * 2048 + lag * 2**22


def opened(code):
    return (
        jnp.bitwise_and(code, 2047),
        jnp.bitwise_and(lax.shift_right_logical(code, 11), 2047),
        lax.shift_right_logical(code, 22),
    )


def pieces(src, code, skip, high_skip, spans):
    low_at, high_at, turn = opened(code)
    return [
        src[pl.ds(low_at + (skip + first), count), :]
        + turned(
            src[pl.ds(high_at + (high_skip + first), count), :],
            src[pl.ds(high_at + (high_skip + first - 1), count), :],
            turn,
        )
        for first, count in spans
    ]


WHOLE = ((0, 8), (8, 8), (16, 1))


def main_kernel(
    x_h, low_h, high_h, lag_h, out, tab, codes, x, low, high, lag, plan, buf_a, buf_b, sems
):
    copies = [
        pltpu.make_async_copy(source, target, sems.at[at])
        for at, (source, target) in enumerate(((low_h, low), (high_h, high), (lag_h, lag)))
    ]
    parts = [
        pltpu.make_async_copy(
            x_h.at[pl.ds(part * 256, 256)], x.at[pl.ds(part * 256, 256)], sems.at[3 + part]
        )
        for part in range(4)
    ]
    for copy in copies + parts:
        copy.start()
    for row in range(ROWS):
        out[pl.ds(row * PACKED, 1), :] = jnp.zeros((1, LANES), F32)
    for row in range(ROWS + 1):
        for buf in (buf_a, buf_b):
            buf[pl.ds(row * PITCH, 8), :] = jnp.zeros((8, LANES), F32)
    for copy in copies:
        copy.wait()
    plan[...] = jnp.zeros_like(plan)
    plan[0:LEVELS, 0:ROWS] = level_codes(low[...], high[...], lag[...])
    planned = pltpu.make_async_copy(plan, codes, sems.at[7])
    planned.start()
    tab[...] = jnp.zeros_like(tab)
    for at, table in enumerate((low, high, lag)):
        tab[pl.ds(2 * at, 2), 0:ROWS] = table[LOCAL + 1 : LEVELS, :]
    none = jnp.zeros((1, LANES), F32)
    for part, copy in enumerate(parts):
        copy.wait()
        for row in range(part * 16, part * 16 + 16, 2):
            at = (row // 8) * 128 + row % 8
            low_row = x[pl.ds(at, CHUNKS, stride=8), :]
            high_row = x[pl.ds(at + 1, CHUNKS, stride=8), :]
            before = jnp.concatenate([none, high_row[: CHUNKS - 1]], axis=0)
            to = row * PITCH + 8
            buf_a[pl.ds(to, CHUNKS), :] = low_row + high_row
            buf_a[pl.ds(to + PITCH, CHUNKS), :] = low_row + turned(high_row, before, 1)
            buf_a[pl.ds(to + PITCH + CHUNKS, 1), :] = turned(none, high_row[CHUNKS - 1 :], 1)
    planned.wait()
    src, dst = buf_a, buf_b
    for level in range(1, LOCAL):
        last = level == LOCAL - 1
        for row in range(ROWS):
            to = row * PACKED + 1 if last else row * PITCH + 8
            for (first, count), piece in zip(WHOLE, pieces(src, codes[level, row], 8, 8, WHOLE)):
                (out if last else dst)[pl.ds(to + first, count), :] = piece
        src, dst = dst, src


def term_codes(tab7, tab8, odd, upper, pitch):
    def rows(tab, at):
        return jnp.broadcast_to(tab[at : at + 1, :], (8, LANES))

    via = jnp.where(upper == 1, rows(tab8, 3), rows(tab8, 1))
    late = jnp.where(upper == 1, rows(tab8, 5), 0)
    source = jnp.where(odd == 1, rows(tab7, 2), rows(tab7, 0))
    later = jnp.where(odd == 1, rows(tab7, 4), 0)
    late = late + jnp.take_along_axis(later, via, axis=1)
    source = jnp.take_along_axis(source, via, axis=1)
    at = source * pitch - lax.shift_right_logical(late, 7)
    return (at * LANES + jnp.bitwise_and(late, LANES - 1))[0:1]


def shares(src, ahead, codes, which, count, put):
    for row in range(ROWS):
        code = codes[which, row]
        at = lax.shift_right_arithmetic(code, 7)
        turn = jnp.bitwise_and(code, LANES - 1)
        for first in range(0, count, 8):
            size = min(8, count - first)
            to = ahead + first
            value = turned(
                src[pl.ds(at + to, size), :], src[pl.ds(at + (to - 1), size), :], turn
            )
            put(row * count + first, size, value)


def into(out):
    def put(at, size, value):
        out[pl.ds(at, size), :] = value

    return put


def core_main_kernel(own, partner, codes, tab, l6, to_pair, to_cross, edge, both):
    core = place()[0]
    size = own.shape[0]
    both[pl.ds(pl.multiple_of(core * size, 8), size), :] = own[...]
    both[pl.ds(pl.multiple_of((1 - core) * size, 8), size), :] = partner[...]
    for message in (to_pair, to_cross):
        message[0:8, :] = tab[...].astype(F32)
    for row in range(ROWS):
        first, second, past = pieces(both, codes[LOCAL, row], 1, size + 1, WHOLE)
        l6[pl.ds(row * CHUNKS, 8), :] = first
        l6[pl.ds(row * CHUNKS + 8, 8), :] = second
        edge[pl.ds(row * 4, 3), :] = second[5:8]
        edge[pl.ds(row * 4 + 3, 1), :] = past
        at = 8 + row * TO_PAIR
        to_pair[pl.ds(at, TO_PAIR - 8), :] = first[PART - 3 :]
        to_pair[pl.ds(at + TO_PAIR - 8, 8), :] = second
        at = 8 + row * TO_CROSS
        to_cross[pl.ds(at, 7), :] = first[1:8]
        to_cross[pl.ds(at + 7, PART - 8), :] = second[0 : PART - 8]


def history_kernel(l6, edge, whole, cross_rest):
    inner = lax.axis_index("tm") > 0
    for row in range(ROWS):
        at = row * WIDE
        ahead = jnp.where(inner, edge[pl.ds(row * 4, 4), :], 0.0)
        block = l6[pl.ds(row * CHUNKS, CHUNKS), :]
        whole[pl.ds(at, 1), :] = jnp.zeros((1, LANES), F32)
        for target, to in ((whole, at + 1), (cross_rest, row * 4)):
            target[pl.ds(to, 3), :] = ahead[0:3]
            target[pl.ds(to + 3, 1), :] = ahead[3:4] + block[0:1]
        whole[pl.ds(at + 5, CHUNKS - 1), :] = block[1:]


def tables_of(message):
    return message[0:8, :].astype(jnp.int32)


def onto(out):
    def put(at, size, value):
        out[pl.ds(at, size), :] += value

    return put


def relay_kernel(l6, pair, cross, for_pair, for_cross, terms, plan, sem):
    _, odd, upper = place()
    pair_tab, cross_tab = tables_of(pair), tables_of(cross)
    plan[...] = jnp.zeros_like(plan)
    plan[0:1, :] = term_codes(cross_tab, pair_tab, 1 - odd, 1 - upper, TO_CROSS)
    plan[1:2, :] = term_codes(pair_tab, cross_tab, 1 - odd, upper, TO_PAIR)
    plan[2:3, :] = term_codes(cross_tab, pair_tab, 1 - odd, 1 - upper, 8)
    plan[3:4, :] = term_codes(pair_tab, pair_tab, odd, upper, CHUNKS)
    plan[4:5, :] = term_codes(pair_tab, cross_tab, odd, upper, CHUNKS)
    plan[5:6, :] = term_codes(pair_tab, pair_tab, odd, upper, WIDE)
    copy = pltpu.make_async_copy(plan, terms, sem)
    copy.start()
    for_pair[ROWS * (PART - 4) :, :] = cross[0:8, :]
    copy.wait()
    shares(cross, 8 + 3, terms, 0, PART - 4, into(for_pair))
    shares(l6, 4, terms, 3, PART - 4, onto(for_pair))
    shares(pair, 8 + 3, terms, 1, 16 - PART, into(for_cross))
    shares(l6, PART, terms, 4, 16 - PART, onto(for_cross))


def first_own_kernel(whole, terms, for_pair):
    shares(whole, 4, terms, 5, 4, into(for_pair))


def first_relay_kernel(own, cross, cross_rest, terms, for_pair, buf):
    for row in range(ROWS):
        buf[pl.ds(row * 8 + 1, 4), :] = cross_rest[pl.ds(row * 4, 4), :]
        buf[pl.ds(row * 8 + 5, 3), :] = cross[pl.ds(8 + row * TO_CROSS, 3), :]

    def put(at, size, value):
        for_pair[pl.ds(at, size), :] = value + own[pl.ds(at, size), :]

    shares(buf, 4, terms, 2, 4, put)


def direct_kernel(whole, pair, cross, cross_rest, tab, relay, out, buf, plan, terms, sem):
    _, odd, upper = place()
    own, other = tab[...], relay[ROWS * (PART - 4) :, :].astype(jnp.int32)
    plan[...] = jnp.zeros_like(plan)
    plan[0:1, :] = term_codes(own, own, odd, upper, WIDE)
    plan[1:2, :] = term_codes(own, own, 1 - odd, upper, TO_PAIR)
    plan[2:3, :] = term_codes(other, own, 1 - odd, 1 - upper, TURN)
    copy = pltpu.make_async_copy(plan, terms, sem)
    copy.start()
    for row in range(ROWS):
        to = row * TURN
        buf[pl.ds(to + 1, 4), :] = cross_rest[pl.ds(row * 4, 4), :]
        buf[pl.ds(to + 5, TO_CROSS), :] = cross[pl.ds(8 + row * TO_CROSS, TO_CROSS), :]
    copy.wait()
    for row in range(ROWS):
        found = []
        for which in range(3):
            code = terms[which, row]
            found.append((lax.shift_right_arithmetic(code, 7), jnp.bitwise_and(code, LANES - 1)))
        (own_at, own_turn), near, away = found
        for first, count, src, ahead, (at, turn) in (
            (0, PART, buf, 4, away),
            (PART, 16 - PART, pair, 8 + 3, near),
        ):
            to = 4 + first
            out[pl.ds(row * CHUNKS + first, count), :] = turned(
                whole[pl.ds(own_at + to, count), :],
                whole[pl.ds(own_at + (to - 1), count), :],
                own_turn,
            ) + turned(
                src[pl.ds(at + ahead, count), :], src[pl.ds(at + (ahead - 1), count), :], turn
            )


def last_kernel(mine, first, second, rest, out, buf, sems):
    copies = []
    for part in range(4):
        for row in range(part * 16, part * 16 + 16):
            at = (row // 8) * 128 + row % 8
            spans = (first, 0, 4), (second, 4, PART - 4), (rest, PART, 16 - PART)
            for arrived, chunk, count in spans:
                value = (
                    mine[pl.ds(row * CHUNKS + chunk, count), :]
                    + arrived[pl.ds(row * count, count), :]
                )
                buf[pl.ds(at + 8 * chunk, count, stride=8), :] = value * SCALE
        here = pl.ds(part * 256, 256)
        copies.append(pltpu.make_async_copy(buf.at[here], out.at[here], sems.at[part]))
        copies[-1].start()
    for copy in copies:
        copy.wait()


def call(kernel, ins, outs, scratch=()):
    pins = {"v": pltpu.VMEM, "t": pltpu.SMEM, "h": pltpu.HBM}
    kinds = {"v": pltpu.VMEM, "t": pltpu.SMEM, "h": pltpu.HBM}
    values = [
        pltpu.with_memory_space_constraint(a, pins[where]) if where in pins else a for a, where in ins
    ]
    return pl.pallas_call(
        kernel,
        out_shape=outs,
        in_specs=[pl.BlockSpec(memory_space=kinds[where]) for _, where in ins],
        out_specs=[pl.BlockSpec(memory_space=getattr(o, "memory_space", pltpu.VMEM)) for o in outs],
        scratch_shapes=list(scratch),
        compiler_params=pltpu.CompilerParams(vmem_limit_bytes=16 * 2**20),
    )(*values)


def pinned(sublanes, lane_count=LANES, dtype=F32):
    return pltpu.VMEM((sublanes, lane_count), dtype)


def swap(bit):
    return [(i, i ^ bit) for i in range(64)]


def on_device(x, low, high, lag):
    tiles = x.reshape(8, 8, CHUNKS, LANES).transpose(0, 2, 1, 3).reshape(1024, LANES)
    sem = pltpu.SemaphoreType.DMA
    ints = jnp.int32
    by_pair, by_cross = swap(2), swap(6)
    plan, terms_ref = pltpu.VMEM((8, LANES), ints), pltpu.SMEM((8, LANES), ints)

    l5, own_tab, codes = call(
        main_kernel,
        [(a, "h") for a in (tiles, low, high, lag)],
        [pinned(ROWS * PACKED), pinned(8, LANES, ints), pltpu.SMEM((16, LANES), ints)],
        [pltpu.VMEM((1024, LANES), F32)]
        + [pltpu.VMEM((LEVELS, ROWS), ints)] * 3
        + [pltpu.VMEM((16, LANES), ints)]
        + [pltpu.VMEM((ROWS * PITCH + 8, LANES), F32)] * 2
        + [sem((8,))],
    )
    l5_far = lax.ppermute(l5, "freq", swap(1))
    l6, pair, cross, edge = call(
        core_main_kernel,
        [(l5, "v"), (l5_far, "v"), (codes, "t"), (own_tab, "v")],
        [pinned(1024), pinned(8 + ROWS * TO_PAIR), pinned(8 + ROWS * TO_CROSS), pinned(ROWS * 4)],
        [pltpu.VMEM((2 * ROWS * PACKED, LANES), F32)],
    )
    cross = lax.ppermute(cross, "freq", by_cross)
    pair = lax.ppermute(pair, "freq", by_pair)
    edge = lax.ppermute(edge, "tm", [(i, (i + 1) % 4) for i in range(4)])

    whole, cross_rest = call(
        history_kernel,
        [(l6, "v"), (edge, "v")],
        [pinned(ROWS * WIDE), pinned(ROWS * 4)],
    )
    cross_rest = lax.ppermute(cross_rest, "freq", by_cross)

    for_pair, for_cross, terms = call(
        relay_kernel,
        [(l6, "v"), (pair, "v"), (cross, "v")],
        [pinned(ROWS * (PART - 4) + 8), pinned(ROWS * (16 - PART)), terms_ref],
        [plan, sem],
    )
    second = lax.ppermute(for_pair, "freq", by_pair)
    rest = lax.ppermute(for_cross, "freq", by_cross)

    (own_first,) = call(first_own_kernel, [(whole, "v"), (terms, "t")], [pinned(ROWS * 4)])
    (for_pair,) = call(
        first_relay_kernel,
        [(own_first, "v"), (cross, "v"), (cross_rest, "v"), (terms, "t")],
        [pinned(ROWS * 4)],
        [pltpu.VMEM((512, LANES), F32)],
    )
    first = lax.ppermute(for_pair, "freq", by_pair)

    (mine,) = call(
        direct_kernel,
        [(a, "v") for a in (whole, pair, cross, cross_rest, own_tab, second)],
        [pinned(ROWS * CHUNKS)],
        [pltpu.VMEM((ROWS * TURN, LANES), F32), plan, terms_ref, sem],
    )
    (out,) = call(
        last_kernel,
        [(a, "v") for a in (mine, first, second, rest)],
        [pltpu.HBM((1024, LANES), F32)],
        [pltpu.VMEM((1024, LANES), F32), sem((4,))],
    )
    return out.reshape(8, CHUNKS, 8, LANES).transpose(0, 2, 1, 3).reshape(ROWS, CHUNKS * LANES)


def solution(mesh):
    placed = (P("freq", "tm"), P(None, "freq"), P(None, "freq"), P(None, "freq"))
    return jax.shard_map(
        on_device, mesh=mesh, in_specs=placed, out_specs=P("freq", "tm"), check_vma=False
    )
```
